32 devices in a mesh: seq: 16 (over z, y, core), mp: 2 (over x).
Axes of the slice: x: 2, y: 2, z: 4, core: 2. Of those that a mesh axis runs over, the one named last changes fastest.
Arguments:
- tokens: bfloat16 [16384, 4096], P('seq', 'mp'), may hold values from -6 to 6
- segment_ids: int32 [16384], P('seq'), may hold values from 0 to 3, never falling along the last dimension, each value on 1 to 8192 neighbouring positions
- w_x: bfloat16 [4096, 4096], P(None, 'mp'), may hold values from -0.09375 to 0.09375
- w_z: bfloat16 [4096, 4096], P(None, 'mp'), may hold values from -0.09375 to 0.09375
- w_bc: bfloat16 [4096, 256], replicated, may hold values from -0.09375 to 0.09375
- w_dt: bfloat16 [4096, 32], P(None, 'mp'), may hold values from -0.09375 to 0.09375
- dt_bias: float32 [32], P('mp'), may hold values from -1 to 1
- rates: float32 [32], P('mp'), may hold values from 3.0517578e-05 to 0.05
- conv_x: float32 [3, 4096], P(None, 'mp'), may hold values from -3 to 3
- conv_bc: float32 [3, 256], replicated, may hold values from -3 to 3
- norm_gain: float32 [4096], P('mp'), may hold values from 0.5 to 1.5
Outputs:
- encoded: bfloat16 [16384, 4096], P('seq', 'mp')
The draws below stay inside these ranges and needn't reach their ends.
Inputs may be any that keep to these rules, and one draw needn't show every extreme that they name: `segment_ids`: document numbers never fall along the slab and start at 0; each document holds 1 to 8192 tokens, and one holds exactly 8192.
All inputs are finite; a program needn't handle non-finite values.
Results may differ from the reference program's by a relative error of at most 0.009.
Values may be sent and summed in bfloat16 or wider, within the bound.
A program may use at most 192 MiB of HBM per device.

```python
import math
import jax
import jax.numpy as jnp
import numpy as np
from jax import lax

D = 4096
HEADS = 32
HEAD_DIM = 128
STATE = 128
INNER = 4096
TOKENS = 16384
BLOCK = 256


def draw_tokens(key, part):
    base_key = jax.random.fold_in(key, 11)
    level_key = jax.random.fold_in(key, 12)
    region_count = TOKENS // BLOCK
    base = jax.random.normal(base_key, (TOKENS, D), jnp.float32)
    shifts = 1.5 * jax.random.normal(level_key, (region_count, D), jnp.float32)
    offsets = jnp.repeat(shifts, BLOCK, axis=0)
    return jnp.clip(base + offsets, -6.0, 6.0).astype(jnp.bfloat16)


def shard_levels(rng, shape, split, smallest, top_value):
    factor_of, own = 1.0, jax.random.fold_in(rng, 6)
    for axis_at, blocks in split:
        heights = jnp.exp(jax.random.uniform(jax.random.fold_in(own, axis_at), (blocks,), jnp.float32, smallest / len(split), top_value / len(split)))
        factor_of = factor_of * jnp.repeat(heights, shape[axis_at] // blocks).reshape([-1 if axis == axis_at else 1 for axis in range(len(shape))])
    return factor_of


def split_up(number_of, total, most, lean):
    weights = [(1 << 20) // math.isqrt(standing ** lean) + 1 for standing in range(2, number_of + 1)]
    spare, counts = total - most - (number_of - 1), [1] * (number_of - 1)
    while spare > 0:
        movable = [i for i in range(number_of - 1) if counts[i] < most]
        whole, remaining = sum([weights[i] for i in movable]), spare
        for i in movable:
            more = min(most - counts[i], max(1, remaining * weights[i] // whole), spare)
            counts[i] = counts[i] + more
            spare = spare - more
    return np.array([most] + counts)


def ragged(key, amount, total, reach, slope):
    if amount == 2:
        one = jax.random.randint(key, (), max(1, total - reach), min(reach, total - 1) + 1)
        return jnp.stack([one, total - one])
    lengths = jnp.asarray(split_up(amount, total, reach, slope), jnp.int32)
    twos = (amount - 1) // 2
    giver, sink = lengths[1:1 + 2 * twos:2], lengths[2:2 + 2 * twos:2]
    margin = jnp.minimum(giver - 1, reach - sink)
    moved = jax.random.randint(jax.random.fold_in(key, 1), (twos,), 0, 1 << 20) % (margin + 1)
    lengths = lengths.at[1:1 + 2 * twos:2].set(giver - moved).at[2:2 + 2 * twos:2].set(sink + moved)
    return lengths[jax.random.permutation(jax.random.fold_in(key, 2), amount)]


def noise(key, dims, deviation, reach, shards=(), held_as=jnp.bfloat16):
    values = deviation * jax.random.normal(key, dims, jnp.float32)
    if shards:
        values = values * shard_levels(key, dims, shards, -0.22, 0.18)
    return jnp.clip(values, -reach, reach).astype(held_as)


def setup_inputs(seed: int = 0) -> dict:
    seeds = jax.random.split(jax.random.key(seed), 12)
    return {
        "tokens": draw_tokens(jax.random.fold_in(seeds[11], 71), 0),
        "segment_ids": jnp.searchsorted(jnp.cumsum(ragged(seeds[1], 4, TOKENS, TOKENS // 2, 0)), jnp.arange(TOKENS), side="right").astype(jnp.int32),
        "w_x": noise(seeds[2], (D, INNER), D ** -0.5, 0.09375, ((1, 2),)),
        "w_z": noise(seeds[3], (D, INNER), D ** -0.5, 0.09375, ((1, 2),)),
        "w_bc": noise(seeds[4], (D, 2 * STATE), D ** -0.5, 0.09375),
        "w_dt": noise(seeds[5], (D, HEADS), D ** -0.5, 0.09375, ((1, 2),)),
        "dt_bias": jnp.clip(jax.random.uniform(seeds[6], (HEADS,), jnp.float32, -1.0, 1.0) * shard_levels(seeds[6], (HEADS,), ((0, 2),), -0.4, 0.0), -1.0, 1.0),
        "rates": jnp.clip(jnp.exp(math.log(0.05) - 7.4014754 * jax.random.uniform(seeds[7], (HEADS,), jnp.float32) ** shard_levels(seeds[7], (HEADS,), ((0, 2),), -0.2, 0.2)), 3.0517578125e-05, 0.05),
        "conv_x": noise(seeds[8], (3, INNER), 0.5, 3.0, ((1, 2),), jnp.float32),
        "conv_bc": noise(seeds[9], (3, 2 * STATE), 0.5, 3.0, (), jnp.float32),
        "norm_gain": jnp.clip(1.0 + 0.1 * jax.random.normal(seeds[10], (INNER,), jnp.float32), 0.5, 1.5),
    }


def rounded(values):
    return lax.optimization_barrier(values.astype(jnp.bfloat16))

def widen(values):
    return lax.optimization_barrier(values).astype(jnp.float32)

def convolve(values, segments, kernel):
    zero_row = jnp.zeros((1, values.shape[1]), jnp.float32)
    padded = jnp.concatenate([zero_row, values, zero_row], axis=0)
    no_doc = jnp.full((1,), -1, jnp.int32)
    seg_pad = jnp.concatenate([no_doc, segments, no_doc])
    before = padded[:-2] * (seg_pad[:-2] == segments)[:, None].astype(jnp.float32)
    after = padded[2:] * (seg_pad[2:] == segments)[:, None].astype(jnp.float32)
    return kernel[0] * before + kernel[1] * values + kernel[2] * after

def sweep(inputs, b_vecs, c_vecs, steps, segments, rates, strict):
    n_tokens = inputs.shape[0]
    n_blocks = n_tokens // BLOCK
    x_blocks = inputs.reshape(n_blocks, BLOCK, HEADS, HEAD_DIM)
    b_blocks = b_vecs.reshape(n_blocks, BLOCK, STATE)
    c_blocks = c_vecs.reshape(n_blocks, BLOCK, STATE)
    dt_blocks = steps.reshape(n_blocks, BLOCK, HEADS)
    seg_blocks = segments.reshape(n_blocks, BLOCK)
    positions = jnp.arange(BLOCK)
    if strict:
        lower_tri = positions[None, :] < positions[:, None]
    else:
        lower_tri = positions[None, :] <= positions[:, None]

    def advance(carry, block_data):
        state_now, seg_prev = carry
        x_blk, b_blk, c_blk, dt_blk, seg_blk = block_data
        cumul = jnp.cumsum(-dt_blk * rates, axis=0)
        keep_mask = (lower_tri & (seg_blk[:, None] == seg_blk[None, :]))[:, :, None]
        gap_sum = cumul[:, None, :] - cumul[None, :, :]
        decay = jnp.where(keep_mask, jnp.exp(jnp.where(keep_mask, gap_sum, 0.0)), 0.0)
        scores = jnp.dot(c_blk, b_blk.T, preferred_element_type=jnp.float32)
        weights = (scores[:, :, None] * decay * dt_blk[None, :, :]).astype(jnp.bfloat16)
        inside = jnp.einsum('ijh,jhp->ihp', widen(weights), x_blk.astype(jnp.float32))
        opening = jnp.where((seg_blk == seg_prev)[:, None], jnp.exp(cumul), 0.0)
        carried = jnp.einsum('in,hpn->ihp', c_blk.astype(jnp.float32), widen(state_now.astype(jnp.bfloat16)))
        carried = carried * opening[:, :, None]
        final_cum = cumul[-1]
        tail_decay = jnp.where((seg_blk == seg_blk[-1])[:, None], jnp.exp(final_cum[None, :] - cumul), 0.0)
        scaled = (x_blk.astype(jnp.float32) * (tail_decay * dt_blk)[:, :, None]).astype(jnp.bfloat16)
        fresh = jnp.einsum('jhp,jn->hpn', widen(scaled), b_blk.astype(jnp.float32))
        block_decay = jnp.exp(final_cum) * (seg_blk[-1] == seg_prev).astype(jnp.float32)
        state_next = block_decay[:, None, None] * state_now + fresh
        return ((state_next, seg_blk[-1]), inside + carried)
    start_state = (jnp.zeros((HEADS, HEAD_DIM, STATE), jnp.float32), jnp.array(-1, jnp.int32))
    _, outputs = lax.scan(advance, start_state, (x_blocks, b_blocks, c_blocks, dt_blocks, seg_blocks))
    return outputs.reshape(n_tokens, HEADS * HEAD_DIM)

def reference(tokens, segment_ids, w_x, w_z, w_bc, w_dt, dt_bias, rates, conv_x, conv_bc, norm_gain):
    proj_x = rounded(jnp.dot(tokens, w_x, preferred_element_type=jnp.float32))
    gate = rounded(jnp.dot(tokens, w_z, preferred_element_type=jnp.float32))
    proj_bc = rounded(jnp.dot(tokens, w_bc, preferred_element_type=jnp.float32))
    steps = jax.nn.softplus(jnp.dot(tokens, w_dt, preferred_element_type=jnp.float32) + dt_bias)
    inputs = rounded(jax.nn.silu(convolve(proj_x.astype(jnp.float32), segment_ids, conv_x)))
    vectors = rounded(jax.nn.silu(convolve(proj_bc.astype(jnp.float32), segment_ids, conv_bc)))
    b_vecs = vectors[:, :STATE]
    c_vecs = vectors[:, STATE:]
    forward = sweep(inputs, b_vecs, c_vecs, steps, segment_ids, rates, False)
    backward = sweep(inputs[::-1], b_vecs[::-1], c_vecs[::-1], steps[::-1], segment_ids[::-1], rates, True)[::-1]
    mixed_y = forward + backward
    gated = mixed_y * jax.nn.silu(gate.astype(jnp.float32))
    scale = lax.rsqrt(lax.optimization_barrier(jnp.mean(gated * gated, axis=1, keepdims=True)) + 1e-05)
    return (gated * scale * norm_gain).astype(jnp.bfloat16)
```

```python
import functools

import jax
import jax.numpy as jnp
from jax import lax
from jax.experimental import pallas as pl
from jax.experimental.pallas import tpu as pltpu
from jax.sharding import PartitionSpec as P

BLOCK = 256
LANES = 128
GROUP = 4
LOG2E = 1.4426950408889634
MESH = pl.DeviceIdType.MESH
VMEM_LIMIT = 60 * 1024 * 1024
F32 = jnp.float32
BF16 = jnp.bfloat16


def silu(v):
    return v / (1.0 + jnp.exp(-v))


def filtered(x, prev, nxt, m_prev, m_next, taps):
    rows = lax.broadcasted_iota(jnp.int32, x.shape, 0)
    last = x.shape[0] - 1
    before = jnp.where(rows == 0, prev, pltpu.roll(x, 1, axis=0)) * m_prev
    after = jnp.where(rows == last, nxt, pltpu.roll(x, last, axis=0)) * m_next
    return silu(taps[0:1] * before + taps[1:2] * x + taps[2:3] * after).astype(BF16)


def local_kernel(
    heads, x_ref, bc_ref, prev_ref, next_ref, raw_ref, bias_ref, rate_ref, aux_ref, seg_ref,
    taps_ref, taps_bc_ref,
    inside_ref, c_ref, opf_ref, opb_ref, sf_ref, sb_ref, dec_ref, tot_ref, totdec_ref,
    accf, accb, run,
):
    step = pl.program_id(0)
    inner = heads * LANES

    @pl.when(step == 0)
    def _():
        accf[...] = jnp.zeros_like(accf)
        accb[...] = jnp.zeros_like(accb)
        run[...] = jnp.ones_like(run)

    aux = aux_ref[...]
    seg_col, m_prev, m_next = aux[:, 0:1], aux[:, 1:2], aux[:, 2:3]
    from_prev, from_next = aux[:, 3:4], aux[:, 4:5]
    with_first, with_last = aux[:, 5:6], aux[:, 6:7]

    raw = raw_ref[...] + bias_ref[...]
    dt = jnp.maximum(raw, 0.0) + jnp.log1p(jnp.exp(-jnp.abs(raw)))
    drop = dt * (rate_ref[...] * -LOG2E)
    row_at = lax.broadcasted_iota(jnp.int32, (BLOCK, BLOCK), 0)
    col_at = lax.broadcasted_iota(jnp.int32, (BLOCK, BLOCK), 1)
    lower = col_at <= row_at
    incl = jnp.dot(lower.astype(F32), drop, precision=lax.Precision.HIGHEST, preferred_element_type=F32)
    excl = jnp.dot((col_at < row_at).astype(F32), drop, precision=lax.Precision.HIGHEST, preferred_element_type=F32)
    total = incl[BLOCK - 1:BLOCK]
    opf_ref[...] = jnp.exp2(incl) * from_prev
    opb_ref[...] = jnp.exp2(total - excl) * from_next
    tail_f = jnp.exp2(total - incl) * with_last * dt
    tail_b = jnp.exp2(excl) * with_first * dt
    whole = jnp.exp2(total)
    dec_f = whole * from_prev[BLOCK - 1:BLOCK]
    dec_b = whole * from_next[0:1]
    dec_ref[0] = jnp.concatenate([dec_f, dec_b, jnp.zeros((6, LANES), F32)], axis=0)
    incl_t, excl_t, dt_t = incl.T, excl.T, dt.T

    bcs = filtered(
        bc_ref[...].astype(F32), prev_ref[0][:, inner:], next_ref[0][:, inner:], m_prev, m_next,
        taps_bc_ref[...],
    )
    c_vecs = bcs[:, LANES:]
    c_ref[...] = c_vecs
    b_t = bcs[:, :LANES].astype(F32).T.astype(BF16)
    scores = jnp.dot(c_vecs, b_t, preferred_element_type=F32)
    scores = jnp.where(seg_col == seg_ref[0], scores, 0.0)

    run_b = run[...]
    for h in range(heads):
        cols = slice(h * LANES, (h + 1) * LANES)
        xs = filtered(
            x_ref[:, cols].astype(F32), prev_ref[0][:, cols], next_ref[0][:, cols], m_prev, m_next,
            taps_ref[:, cols],
        )
        one = slice(h, h + 1)
        gap = jnp.where(lower, incl[:, one] - incl_t[one], excl_t[one] - excl[:, one])
        weights = (scores * jnp.exp2(gap) * dt_t[one]).astype(BF16)
        inside_ref[:, cols] = jnp.dot(weights, xs, preferred_element_type=F32)
        wide = xs.astype(F32)
        fresh_f = jnp.dot(b_t, (wide * tail_f[:, one]).astype(BF16), preferred_element_type=F32)
        fresh_b = jnp.dot(b_t, (wide * tail_b[:, one]).astype(BF16), preferred_element_type=F32)
        sf_ref[0, :, cols] = fresh_f
        sb_ref[0, :, cols] = fresh_b
        accf[:, cols] = accf[:, cols] * dec_f[:, one] + fresh_f
        accb[:, cols] = accb[:, cols] + run_b[1:2, one] * fresh_b
    run[...] = run_b * dec_ref[0]

    @pl.when(step == pl.num_programs(0) - 1)
    def _():
        part = LANES // GROUP
        for q in range(GROUP):
            tot_ref[q, 0] = accf[q * part:(q + 1) * part, :].astype(BF16)
            tot_ref[q, 1] = accb[q * part:(q + 1) * part, :].astype(BF16)
        totdec_ref[...] = run_b * dec_ref[0]


def local_part(xp, bc, prev, nxt, raw, bias, rate, aux, seg_rows, taps, taps_bc, heads):
    tok, inner = xp.shape
    blocks = tok // BLOCK
    part = LANES // GROUP
    row = lambda b: (b, 0)
    lead = lambda b: (b, 0, 0)
    fixed = lambda b: (0, 0)
    flops = tok * heads * (2 * BLOCK * LANES + 4 * LANES * LANES)
    return pl.pallas_call(
        functools.partial(local_kernel, heads),
        grid=(blocks,),
        in_specs=[
            pl.BlockSpec((BLOCK, inner), row),
            pl.BlockSpec((BLOCK, 2 * LANES), row),
            pl.BlockSpec((1, 1, inner + 2 * LANES), lead),
            pl.BlockSpec((1, 1, inner + 2 * LANES), lead),
            pl.BlockSpec((BLOCK, LANES), row),
            pl.BlockSpec((1, LANES), fixed),
            pl.BlockSpec((1, LANES), fixed),
            pl.BlockSpec((BLOCK, 8), row),
            pl.BlockSpec((1, 1, BLOCK), lead),
            pl.BlockSpec((3, inner), fixed),
            pl.BlockSpec((3, 2 * LANES), fixed),
        ],
        out_specs=[
            pl.BlockSpec((BLOCK, inner), row),
            pl.BlockSpec((BLOCK, LANES), row),
            pl.BlockSpec((BLOCK, LANES), row),
            pl.BlockSpec((BLOCK, LANES), row),
            pl.BlockSpec((1, LANES, inner), lead),
            pl.BlockSpec((1, LANES, inner), lead),
            pl.BlockSpec((1, 8, LANES), lead),
            pl.BlockSpec((GROUP, 2, part, inner), lambda b: (0, 0, 0, 0)),
            pl.BlockSpec((8, LANES), fixed),
        ],
        out_shape=[
            jax.ShapeDtypeStruct((tok, inner), F32),
            jax.ShapeDtypeStruct((tok, LANES), BF16),
            jax.ShapeDtypeStruct((tok, LANES), F32),
            jax.ShapeDtypeStruct((tok, LANES), F32),
            jax.ShapeDtypeStruct((blocks, LANES, inner), F32),
            jax.ShapeDtypeStruct((blocks, LANES, inner), F32),
            jax.ShapeDtypeStruct((blocks, 8, LANES), F32),
            jax.ShapeDtypeStruct((GROUP, 2, part, inner), BF16),
            jax.ShapeDtypeStruct((8, LANES), F32),
        ],
        scratch_shapes=[
            pltpu.VMEM((LANES, inner), F32),
            pltpu.VMEM((LANES, inner), F32),
            pltpu.VMEM((8, LANES), F32),
        ],
        compiler_params=pltpu.CompilerParams(
            dimension_semantics=("arbitrary",), vmem_limit_bytes=VMEM_LIMIT
        ),
        cost_estimate=pl.CostEstimate(
            flops=flops, bytes_accessed=tok * inner * 6 + 4 * inner * LANES * 8,
            transcendentals=tok * BLOCK * heads,
        ),
        name="local_part",
    )(xp, bc, prev, nxt, raw, bias, rate, aux, seg_rows, taps, taps_bc)


def spread(row, heads):
    return jnp.concatenate(
        [jnp.broadcast_to(row[:, h:h + 1], (1, LANES)) for h in range(heads)], axis=1
    )


def product(terms):
    out = terms[0]
    for term in terms[1:]:
        out = out * term
    return out


def exchange_kernel(
    heads, zs, tot_ref, dec_ref, ent_ref,
    near, near_dec, sums, sums_dec, far_f, far_b, far_dec, back, landed,
    near_s, near_r, dec_s, dec_r, f_s, f_r, b_s, b_r, fd_s, fd_r, back_s, back_r,
):
    me = lax.axis_index("seq")
    i = lax.rem(me, GROUP)
    z = lax.div(me, GROUP)
    low, high = lax.rem(i, 2), lax.div(i, 2)
    members = [i]
    for r in range(1, GROUP):
        other_low = 1 - low if r % 2 else low
        other_high = 1 - high if r // 2 else high
        members.append(other_high * 2 + other_low)
    far_dec[...] = jnp.ones_like(far_dec)
    far_f[...] = jnp.zeros_like(far_f)
    far_b[...] = jnp.zeros_like(far_b)

    barrier = pltpu.get_barrier_semaphore()
    for r in range(1, GROUP):
        pl.semaphore_signal(
            barrier, inc=1, device_id={"seq": z * GROUP + members[r]}, device_id_type=MESH
        )
    for d in range(1, zs):
        pl.semaphore_signal(
            barrier, inc=1, device_id={"seq": lax.rem(z + d, zs) * GROUP + i}, device_id_type=MESH
        )
    pl.semaphore_wait(barrier, GROUP - 1 + zs - 1)

    def send(src, dst, ssem, rsem, to):
        return pltpu.make_async_remote_copy(
            src_ref=src, dst_ref=dst, send_sem=ssem, recv_sem=rsem,
            device_id={"seq": to}, device_id_type=MESH,
        )

    firsts = []
    for r in range(1, GROUP):
        to = z * GROUP + members[r]
        firsts.append(send(dec_ref, near_dec.at[r], dec_s.at[r], dec_r.at[r], to))
        firsts.append(send(tot_ref.at[members[r]], near.at[r], near_s.at[r], near_r.at[r], to))
    for copy in firsts:
        copy.start()
    for copy in firsts:
        copy.wait()

    decs = [dec_ref[...]] + [near_dec[r] for r in range(1, GROUP)]

    def state(r, way):
        value = tot_ref[i, way] if r == 0 else near[r, way]
        return value.astype(F32)

    def between(r, s, way):
        terms = []
        for k in range(GROUP):
            if way == 0:
                inside = (members[k] > members[r]) & (members[k] < members[s])
            else:
                inside = (members[k] < members[r]) & (members[k] > members[s])
            terms.append(jnp.where(inside, decs[k][way:way + 1], 1.0))
        return product(terms)

    def beyond(r, way):
        terms = []
        for k in range(GROUP):
            if way == 0:
                inside = members[k] > members[r]
            else:
                inside = members[k] < members[r]
            terms.append(jnp.where(inside, decs[k][way:way + 1], 1.0))
        return product(terms)

    for way in range(2):
        total = jnp.zeros(sums.shape[1:], F32)
        for r in range(GROUP):
            total = total + spread(beyond(r, way), heads) * state(r, way)
        sums[way] = total.astype(BF16)
    sums_dec[...] = product(decs)

    for d in range(1, zs):
        up = (z + d) * GROUP + i
        down = (z - d) * GROUP + i

        @pl.when(z + d < zs)
        def _():
            send(sums_dec, far_dec.at[0, d], fd_s.at[0, d], fd_r.at[0, d], up).start()
            send(sums.at[0], far_f.at[d], f_s.at[d], f_r.at[d], up).start()

        @pl.when(z - d >= 0)
        def _():
            send(sums_dec, far_dec.at[1, d], fd_s.at[1, d], fd_r.at[1, d], down).start()
            send(sums.at[1], far_b.at[d], b_s.at[d], b_r.at[d], down).start()

    for d in range(1, zs):
        up = (z + d) * GROUP + i
        down = (z - d) * GROUP + i

        @pl.when(z - d >= 0)
        def _():
            send(sums_dec, far_dec.at[0, d], fd_s.at[0, d], fd_r.at[0, d], down).wait_recv()
            send(sums.at[0], far_f.at[d], f_s.at[d], f_r.at[d], down).wait_recv()

        @pl.when(z + d < zs)
        def _():
            send(sums_dec, far_dec.at[1, d], fd_s.at[1, d], fd_r.at[1, d], up).wait_recv()
            send(sums.at[1], far_b.at[d], b_s.at[d], b_r.at[d], up).wait_recv()

    for way in range(2):
        far = far_b if way else far_f
        entering = jnp.zeros(sums.shape[1:], F32)
        weight = jnp.ones((1, LANES), F32)
        for d in range(1, zs):
            entering = entering + spread(weight, heads) * far[d].astype(F32)
            weight = weight * far_dec[way, d][way:way + 1]
        for s in range(GROUP):
            terms = []
            for k in range(GROUP):
                if way == 0:
                    earlier = members[k] < members[s]
                else:
                    earlier = members[k] > members[s]
                terms.append(jnp.where(earlier, decs[k][way:way + 1], 1.0))
            value = spread(product(terms), heads) * entering
            for r in range(GROUP):
                if r != s:
                    if way == 0:
                        earlier = members[r] < members[s]
                    else:
                        earlier = members[r] > members[s]
                    weight = jnp.where(earlier, between(r, s, way), 0.0)
                    value = value + spread(weight, heads) * state(r, way)
            back[s, way] = value.astype(BF16)

    lasts = []
    for r in range(1, GROUP):
        to = z * GROUP + members[r]
        lasts.append(send(back.at[r], landed.at[r], back_s.at[r], back_r.at[r], to))
    for copy in lasts:
        copy.start()
    ent_ref[i] = back[0]
    for r in range(1, GROUP):
        lasts[r - 1].wait()
        ent_ref[members[r]] = landed[r]

    for d in range(1, zs):
        up = (z + d) * GROUP + i
        down = (z - d) * GROUP + i

        @pl.when(z + d < zs)
        def _():
            send(sums_dec, far_dec.at[0, d], fd_s.at[0, d], fd_r.at[0, d], up).wait_send()
            send(sums.at[0], far_f.at[d], f_s.at[d], f_r.at[d], up).wait_send()

        @pl.when(z - d >= 0)
        def _():
            send(sums_dec, far_dec.at[1, d], fd_s.at[1, d], fd_r.at[1, d], down).wait_send()
            send(sums.at[1], far_b.at[d], b_s.at[d], b_r.at[d], down).wait_send()


def exchange(tot, totdec, heads):
    zs = lax.axis_size("seq") // GROUP
    _, _, part, inner = tot.shape
    dma = pltpu.SemaphoreType.DMA
    vmem = pl.BlockSpec(memory_space=pltpu.VMEM)
    return pl.pallas_call(
        functools.partial(exchange_kernel, heads, zs),
        in_specs=[vmem, vmem],
        out_specs=vmem,
        out_shape=jax.ShapeDtypeStruct(tot.shape, BF16),
        scratch_shapes=[
            pltpu.VMEM((GROUP, 2, part, inner), BF16),
            pltpu.VMEM((GROUP, 8, LANES), F32),
            pltpu.VMEM((2, part, inner), BF16),
            pltpu.VMEM((8, LANES), F32),
            pltpu.VMEM((zs, part, inner), BF16),
            pltpu.VMEM((zs, part, inner), BF16),
            pltpu.VMEM((2, zs, 8, LANES), F32),
            pltpu.VMEM((GROUP, 2, part, inner), BF16),
            pltpu.VMEM((GROUP, 2, part, inner), BF16),
            dma((GROUP,)), dma((GROUP,)), dma((GROUP,)), dma((GROUP,)),
            dma((zs,)), dma((zs,)), dma((zs,)), dma((zs,)),
            dma((2, zs)), dma((2, zs)),
            dma((GROUP,)), dma((GROUP,)),
        ],
        compiler_params=pltpu.CompilerParams(
            collective_id=1, has_side_effects=True, vmem_limit_bytes=VMEM_LIMIT
        ),
        cost_estimate=pl.CostEstimate(
            flops=tot.size * 20, bytes_accessed=tot.size * 8, transcendentals=0
        ),
        name="exchange_states",
    )(tot, totdec)


def finish_kernel(
    heads, inside_ref, c_ref, opf_ref, opb_ref, gate_ref, sf_ref, sb_ref, dec_ref, decs_ref,
    ent_ref, out_ref, sq_ref, hf, hb,
):
    step = pl.program_id(0)
    blocks = hb.shape[0]
    part = LANES // GROUP

    @pl.when(step == 0)
    def _():
        for q in range(GROUP):
            hf[q * part:(q + 1) * part, :] = ent_ref[q, 0].astype(F32)
        for h in range(heads):
            cols = slice(h * LANES, (h + 1) * LANES)
            now = jnp.concatenate([ent_ref[q, 1, :, cols] for q in range(GROUP)], axis=0).astype(F32)
            for b in range(blocks - 1, -1, -1):
                hb[b, :, cols] = now.astype(BF16)
                if b:
                    now = now * decs_ref[b, 1:2, h:h + 1] + sb_ref[b, :, cols]

    c_vecs = c_ref[...]
    opf, opb = opf_ref[...], opb_ref[...]
    squares = jnp.zeros((BLOCK, LANES), F32)
    for h in range(heads):
        cols = slice(h * LANES, (h + 1) * LANES)
        one = slice(h, h + 1)
        state = hf[:, cols]
        got_f = jnp.dot(c_vecs, state.astype(BF16), preferred_element_type=F32)
        got_b = jnp.dot(c_vecs, hb[step, :, cols], preferred_element_type=F32)
        hf[:, cols] = state * dec_ref[0, 0:1, one] + sf_ref[0, :, cols]
        mixed = inside_ref[:, cols] + got_f * opf[:, one] + got_b * opb[:, one]
        gated = mixed * silu(gate_ref[:, cols].astype(F32))
        squares = squares + gated * gated
        out_ref[:, cols] = gated
    sq_ref[...] = jnp.sum(squares, axis=1, keepdims=True)


def finish(inside, c_vecs, opf, opb, gate, sf, sb, dec, ent, heads):
    tok, inner = inside.shape
    blocks = tok // BLOCK
    part = LANES // GROUP
    row = lambda b: (b, 0)
    lead = lambda b: (b, 0, 0)
    whole = lambda b: (0, 0, 0)
    return pl.pallas_call(
        functools.partial(finish_kernel, heads),
        grid=(blocks,),
        in_specs=[
            pl.BlockSpec((BLOCK, inner), row),
            pl.BlockSpec((BLOCK, LANES), row),
            pl.BlockSpec((BLOCK, LANES), row),
            pl.BlockSpec((BLOCK, LANES), row),
            pl.BlockSpec((BLOCK, inner), row),
            pl.BlockSpec((1, LANES, inner), lead),
            pl.BlockSpec((blocks, LANES, inner), whole),
            pl.BlockSpec((1, 8, LANES), lead),
            pl.BlockSpec((blocks, 8, LANES), whole),
            pl.BlockSpec((GROUP, 2, part, inner), lambda b: (0, 0, 0, 0)),
        ],
        out_specs=[pl.BlockSpec((BLOCK, inner), row), pl.BlockSpec((BLOCK, 1), row)],
        out_shape=[
            jax.ShapeDtypeStruct((tok, inner), F32),
            jax.ShapeDtypeStruct((tok, 1), F32),
        ],
        scratch_shapes=[
            pltpu.VMEM((LANES, inner), F32),
            pltpu.VMEM((blocks, LANES, inner), BF16),
        ],
        compiler_params=pltpu.CompilerParams(
            dimension_semantics=("arbitrary",), vmem_limit_bytes=VMEM_LIMIT
        ),
        cost_estimate=pl.CostEstimate(
            flops=tok * inner * LANES * 4, bytes_accessed=tok * inner * 10, transcendentals=tok * inner
        ),
        name="finish",
    )(inside, c_vecs, opf, opb, gate, sf, sb, dec, dec, ent)


def neighbours(rows):
    count = lax.axis_size("seq")
    from_left = lax.ppermute(rows[-1:], "seq", [(i, i + 1) for i in range(count - 1)])
    from_right = lax.ppermute(rows[:1], "seq", [(i + 1, i) for i in range(count - 1)])
    return from_left, from_right


def shards(tokens, segment_ids, w_x, w_z, w_bc, w_dt, dt_bias, rates, conv_x, conv_bc, norm_gain):
    tok = tokens.shape[0]
    inner = w_x.shape[1]
    heads = w_dt.shape[1]
    mp_count = lax.axis_size("mp")
    seq_count = lax.axis_size("seq")
    position = lax.axis_index("seq")
    blocks = tok // BLOCK

    seg = segment_ids.astype(F32)
    seg_left, seg_right = neighbours(seg)
    seg_left = jnp.where(position > 0, seg_left, -1.0)
    seg_right = jnp.where(position < seq_count - 1, seg_right, -1.0)
    before = jnp.concatenate([seg_left, seg[:-1]])
    after = jnp.concatenate([seg[1:], seg_right])
    by_block = lambda v: jnp.repeat(v, BLOCK)
    aux = jnp.stack(
        [
            seg,
            (seg == before).astype(F32),
            (seg == after).astype(F32),
            (seg == by_block(before[::BLOCK])).astype(F32),
            (seg == by_block(after[BLOCK - 1::BLOCK])).astype(F32),
            (seg == by_block(seg[::BLOCK])).astype(F32),
            (seg == by_block(seg[BLOCK - 1::BLOCK])).astype(F32),
            seg,
        ],
        axis=1,
    )
    seg_rows = seg.reshape(blocks, 1, BLOCK)
    w_small = jnp.concatenate([w_bc, jnp.pad(w_dt, ((0, 0), (0, LANES - heads)))], axis=1)
    bias = jnp.pad(dt_bias, (0, LANES - heads))[None]
    rate = jnp.pad(rates, (0, LANES - heads))[None]

    piece = lax.all_gather(tokens, "mp", axis=1, tiled=True)
    small = jnp.dot(piece, w_small, preferred_element_type=F32)
    bc = small[:, :2 * LANES].astype(BF16)
    raw = small[:, 2 * LANES:]
    xp = jnp.dot(piece, w_x, preferred_element_type=F32).astype(BF16)
    gate = jnp.dot(piece, w_z, preferred_element_type=F32).astype(BF16)

    firsts = jnp.concatenate([xp[::BLOCK], bc[::BLOCK]], axis=1).astype(F32)
    lasts = jnp.concatenate([xp[BLOCK - 1::BLOCK], bc[BLOCK - 1::BLOCK]], axis=1).astype(F32)
    from_left = lax.ppermute(lasts[-1:], "seq", [(i, i + 1) for i in range(seq_count - 1)])
    from_right = lax.ppermute(firsts[:1], "seq", [(i + 1, i) for i in range(seq_count - 1)])
    prev = jnp.concatenate([from_left, lasts[:-1]], axis=0)[:, None]
    nxt = jnp.concatenate([firsts[1:], from_right], axis=0)[:, None]

    inside, c_vecs, opf, opb, sf, sb, dec, tot, totdec = local_part(
        xp, bc, prev, nxt, raw, bias, rate, aux, seg_rows, conv_x, conv_bc, heads
    )
    ent = exchange(tot, totdec, heads)
    gated, sq = finish(inside, c_vecs, opf, opb, gate, sf, sb, dec, ent, heads)
    squares = lax.psum(sq, "mp")
    scale = lax.rsqrt(squares / (inner * mp_count) + 1e-05)
    return (gated * scale * norm_gain).astype(BF16)


def solution(mesh):
    placed = (
        P("seq", "mp"),
        P("seq"),
        P(None, "mp"),
        P(None, "mp"),
        P(),
        P(None, "mp"),
        P("mp"),
        P("mp"),
        P(None, "mp"),
        P(),
        P("mp"),
    )
    return jax.shard_map(
        shards, mesh=mesh, in_specs=placed, out_specs=P("seq", "mp"), check_vma=False
    )
```

```python
import functools

import jax
import jax.numpy as jnp
from jax import lax
from jax.experimental import pallas as pl
from jax.experimental.pallas import tpu as pltpu
from jax.sharding import PartitionSpec as P

BLOCK = 256
LANES = 128
GROUP = 4
LOG2E = 1.4426950408889634
MESH = pl.DeviceIdType.MESH
VMEM_LIMIT = 60 * 1024 * 1024
F32 = jnp.float32
BF16 = jnp.bfloat16


TILE = 512


def project_kernel(
    mp, seqs, tok_ref, wx_ref, wz_ref, ws_ref,
    xp_ref, gate_ref, bc_ref, raw_ref, halo_ref,
    tok_v, wx_v, wz_v, ws_v, acc_x, acc_z, acc_s, stage_x, stage_z, edges, landed,
    own_sem, w_sem, send_sem, recv_sem, out_sem, edge_s, edge_r,
):
    me = lax.axis_index("mp")
    at = lax.axis_index("seq")
    tok, width = tok_ref.shape
    chunks = tok // BLOCK
    order = [0, chunks - 1] + list(range(1, chunks - 1))

    def rows(c):
        return pl.ds(c * BLOCK, BLOCK)

    loads = [
        pltpu.make_async_copy(src, dst, w_sem.at[n])
        for n, (src, dst) in enumerate(((wx_ref, wx_v), (ws_ref, ws_v), (wz_ref, wz_v)))
    ]
    owns = [
        pltpu.make_async_copy(tok_ref.at[rows(c)], tok_v.at[me, rows(c)], own_sem.at[c])
        for c in range(chunks)
    ]
    barrier = pltpu.get_barrier_semaphore()
    for k in range(1, mp):
        pl.semaphore_signal(
            barrier, inc=1, device_id={"mp": lax.rem(me + k, mp)}, device_id_type=MESH
        )

    for other in (lax.rem(at + 1, seqs), lax.rem(at + seqs - 1, seqs)):
        pl.semaphore_signal(barrier, inc=1, device_id={"seq": other}, device_id_type=MESH)
    owns[order[0]].start()
    loads[0].start()
    pl.semaphore_wait(barrier, mp - 1 + 2)

    def sends(c):
        return [
            pltpu.make_async_remote_copy(
                src_ref=tok_ref.at[rows(c)], dst_ref=tok_v.at[me, rows(c)],
                send_sem=send_sem.at[k, c], recv_sem=recv_sem.at[k, c],
                device_id={"mp": lax.rem(me + k, mp)}, device_id_type=MESH,
            )
            for k in range(1, mp)
        ]

    def arrival(c, k):
        source = lax.rem(me - k + mp, mp)
        return source, pltpu.make_async_remote_copy(
            src_ref=tok_ref.at[rows(c)], dst_ref=tok_v.at[source, rows(c)],
            send_sem=send_sem.at[k, c], recv_sem=recv_sem.at[k, c],
            device_id={"mp": source}, device_id_type=MESH,
        )

    def edge(way, to):
        return pltpu.make_async_remote_copy(
            src_ref=edges.at[way], dst_ref=landed.at[way],
            send_sem=edge_s.at[way], recv_sem=edge_r.at[way],
            device_id={"seq": to}, device_id_type=MESH,
        )

    going = sends(order[0])
    for copy in going:
        copy.start()
    loads[1].start()
    loads[2].start()
    for c in order[1:]:
        owns[c].start()

    def out(c, slot, which):
        stage, to = (stage_x, xp_ref) if which == 0 else (stage_z, gate_ref)
        return pltpu.make_async_copy(stage.at[slot], to.at[rows(c)], out_sem.at[which, slot])

    for n, c in enumerate(order):
        slot = n % 2

        def contract(source, weights, acc, stage, first, last):
            depth = pl.ds(pl.multiple_of(source * width, width), width)
            tile = min(TILE, weights.shape[1])

            @pl.loop(0, weights.shape[1] // tile)
            def _(t):
                cols = pl.ds(pl.multiple_of(t * tile, tile), tile)
                part = jnp.dot(
                    tok_v[source, rows(c), :], weights[depth, cols], preferred_element_type=F32
                )
                if not first:
                    part = part + acc[:, cols]
                if last:
                    stage[slot, :, cols] = part.astype(BF16)
                else:
                    acc[:, cols] = part

        def contract_small(source, first):
            depth = pl.ds(pl.multiple_of(source * width, width), width)
            part = jnp.dot(tok_v[source, rows(c), :], ws_v[depth, :], preferred_element_type=F32)
            acc_s[...] = part if first else acc_s[...] + part

        owns[c].wait()
        if n == 0:
            loads[0].wait()
        contract(me, wx_v, acc_x, stage_x, True, False)
        if n == 0:
            loads[1].wait()
        contract_small(me, True)
        if n == 0:
            loads[2].wait()
        contract(me, wz_v, acc_z, stage_z, True, False)
        for copy in going:
            copy.wait_send()
        if n + 1 < chunks:
            going = sends(order[n + 1])
            for copy in going:
                copy.start()
        if n >= 2:
            for which in range(2):
                out(order[n - 2], slot, which).wait()
        sources = []
        for k in range(1, mp):
            source, copy = arrival(c, k)
            copy.wait_recv()
            sources.append(source)
            contract(source, wx_v, acc_x, stage_x, False, k == mp - 1)
            contract_small(source, False)
        out(c, slot, 0).start()
        bc_ref[rows(c), :] = acc_s[:, :2 * LANES].astype(BF16)
        raw_ref[rows(c), :] = acc_s[:, 2 * LANES:]
        inner = stage_x.shape[2]
        if n == 0:
            edges[0, :, :inner] = stage_x[slot, :16, :]
            edges[0, :, inner:] = acc_s[:16, :2 * LANES].astype(BF16)
        if n == 1:
            edges[1, :, :inner] = stage_x[slot, BLOCK - 16:, :]
            edges[1, :, inner:] = acc_s[BLOCK - 16:, :2 * LANES].astype(BF16)

            @pl.when(at > 0)
            def _():
                edge(0, at - 1).start()

            @pl.when(at < seqs - 1)
            def _():
                edge(1, at + 1).start()

        for k, source in enumerate(sources):
            contract(source, wz_v, acc_z, stage_z, False, k == mp - 2)
        out(c, slot, 1).start()

    @pl.when(at > 0)
    def _():
        edge(1, at - 1).wait_recv()
        halo_ref[0] = landed[1]
        edge(0, at - 1).wait_send()

    @pl.when(at == 0)
    def _():
        halo_ref[0] = jnp.zeros(halo_ref.shape[1:], BF16)

    @pl.when(at < seqs - 1)
    def _():
        edge(0, at + 1).wait_recv()
        halo_ref[1] = landed[0]
        edge(1, at + 1).wait_send()

    @pl.when(at == seqs - 1)
    def _():
        halo_ref[1] = jnp.zeros(halo_ref.shape[1:], BF16)

    for n in range(max(0, chunks - 2), chunks):
        for which in range(2):
            out(order[n], n % 2, which).wait()


def project(tokens, w_x, w_z, w_small):
    tok, width = tokens.shape
    inner = w_x.shape[1]
    mp = lax.axis_size("mp")
    seqs = lax.axis_size("seq")
    chunks = tok // BLOCK
    dma = pltpu.SemaphoreType.DMA
    anywhere = pl.BlockSpec(memory_space=pl.ANY)
    vmem = pl.BlockSpec(memory_space=pltpu.VMEM)
    small = w_small.shape[1]
    return pl.pallas_call(
        functools.partial(project_kernel, mp, seqs),
        in_specs=[anywhere] * 4,
        out_specs=[anywhere, anywhere, vmem, vmem, vmem],
        out_shape=[
            jax.ShapeDtypeStruct((tok, inner), BF16),
            jax.ShapeDtypeStruct((tok, inner), BF16),
            jax.ShapeDtypeStruct((tok, 2 * LANES), BF16),
            jax.ShapeDtypeStruct((tok, small - 2 * LANES), F32),
            jax.ShapeDtypeStruct((2, 16, inner + 2 * LANES), BF16),
        ],
        scratch_shapes=[
            pltpu.VMEM((mp, tok, width), BF16),
            pltpu.VMEM(w_x.shape, BF16),
            pltpu.VMEM(w_z.shape, BF16),
            pltpu.VMEM(w_small.shape, BF16),
            pltpu.VMEM((BLOCK, inner), F32),
            pltpu.VMEM((BLOCK, inner), F32),
            pltpu.VMEM((BLOCK, small), F32),
            pltpu.VMEM((2, BLOCK, inner), BF16),
            pltpu.VMEM((2, BLOCK, inner), BF16),
            pltpu.VMEM((2, 16, inner + 2 * LANES), BF16),
            pltpu.VMEM((2, 16, inner + 2 * LANES), BF16),
            dma((chunks,)), dma((3,)), dma((mp, chunks)), dma((mp, chunks)), dma((2, 2)),
            dma((2,)), dma((2,)),
        ],
        compiler_params=pltpu.CompilerParams(
            collective_id=2, has_side_effects=True, vmem_limit_bytes=VMEM_LIMIT
        ),
        cost_estimate=pl.CostEstimate(
            flops=2 * tok * width * mp * (2 * inner + small),
            bytes_accessed=width * mp * (2 * inner + small) * 2, transcendentals=0,
        ),
        name="gather_and_project",
    )(tokens, w_x, w_z, w_small)


def silu(v):
    return v / (1.0 + jnp.exp(-v))


def filtered(x, prev, nxt, m_prev, m_next, taps):
    rows = lax.broadcasted_iota(jnp.int32, x.shape, 0)
    last = x.shape[0] - 1
    before = jnp.where(rows == 0, prev, pltpu.roll(x, 1, axis=0)) * m_prev
    after = jnp.where(rows == last, nxt, pltpu.roll(x, last, axis=0)) * m_next
    return silu(taps[0:1] * before + taps[1:2] * x + taps[2:3] * after).astype(BF16)


def local_kernel(
    heads, x_ref, bc_ref, xl_ref, xr_ref, bl_ref, br_ref, halo_ref, raw_ref, bias_ref, rate_ref, aux_ref, seg_ref,
    taps_ref, taps_bc_ref,
    inside_ref, c_ref, opf_ref, opb_ref, sf_ref, sb_ref, dec_ref, tot_ref, totdec_ref,
    accf, accb, run,
):
    step = pl.program_id(0)
    inner = heads * LANES

    @pl.when(step == 0)
    def _():
        accf[...] = jnp.zeros_like(accf)
        accb[...] = jnp.zeros_like(accb)
        run[...] = jnp.ones_like(run)

    at_left = step == 0
    at_right = step == pl.num_programs(0) - 1

    def beside(left, right, cols):
        left_halo, right_halo = halo_ref[0, :, cols], halo_ref[1, :, cols]
        prev = jnp.where(at_left, left_halo.astype(F32), left.astype(F32))[15:16]
        nxt = jnp.where(at_right, right_halo.astype(F32), right.astype(F32))[0:1]
        return prev, nxt

    aux = aux_ref[...]
    seg_col, m_prev, m_next = aux[:, 0:1], aux[:, 1:2], aux[:, 2:3]
    from_prev, from_next = aux[:, 3:4], aux[:, 4:5]
    with_first, with_last = aux[:, 5:6], aux[:, 6:7]

    raw = raw_ref[...] + bias_ref[...]
    dt = jnp.maximum(raw, 0.0) + jnp.log1p(jnp.exp(-jnp.abs(raw)))
    drop = dt * (rate_ref[...] * -LOG2E)
    row_at = lax.broadcasted_iota(jnp.int32, (BLOCK, BLOCK), 0)
    col_at = lax.broadcasted_iota(jnp.int32, (BLOCK, BLOCK), 1)
    lower = col_at <= row_at
    incl = jnp.dot(lower.astype(F32), drop, precision=lax.Precision.HIGHEST, preferred_element_type=F32)
    excl = jnp.dot((col_at < row_at).astype(F32), drop, precision=lax.Precision.HIGHEST, preferred_element_type=F32)
    total = incl[BLOCK - 1:BLOCK]
    opf_ref[...] = jnp.exp2(incl) * from_prev
    opb_ref[...] = jnp.exp2(total - excl) * from_next
    tail_f = jnp.exp2(total - incl) * with_last * dt
    tail_b = jnp.exp2(excl) * with_first * dt
    whole = jnp.exp2(total)
    dec_f = whole * from_prev[BLOCK - 1:BLOCK]
    dec_b = whole * from_next[0:1]
    dec_ref[0] = jnp.concatenate([dec_f, dec_b, jnp.zeros((6, LANES), F32)], axis=0)
    incl_t, excl_t, dt_t = incl.T, excl.T, dt.T

    prev, nxt = beside(bl_ref[...], br_ref[...], slice(inner, inner + 2 * LANES))
    bcs = filtered(bc_ref[...].astype(F32), prev, nxt, m_prev, m_next, taps_bc_ref[...])
    c_vecs = bcs[:, LANES:]
    c_ref[...] = c_vecs
    b_t = bcs[:, :LANES].astype(F32).T.astype(BF16)
    scores = jnp.dot(c_vecs, b_t, preferred_element_type=F32)
    scores = jnp.where(seg_col == seg_ref[0], scores, 0.0)

    run_b = run[...]
    for h in range(heads):
        cols = slice(h * LANES, (h + 1) * LANES)
        prev, nxt = beside(xl_ref[:, cols], xr_ref[:, cols], cols)
        xs = filtered(x_ref[:, cols].astype(F32), prev, nxt, m_prev, m_next, taps_ref[:, cols])
        one = slice(h, h + 1)
        gap = jnp.where(lower, incl[:, one] - incl_t[one], excl_t[one] - excl[:, one])
        weights = (scores * jnp.exp2(gap) * dt_t[one]).astype(BF16)
        inside_ref[:, cols] = jnp.dot(weights, xs, preferred_element_type=F32)
        wide = xs.astype(F32)
        fresh_f = jnp.dot(b_t, (wide * tail_f[:, one]).astype(BF16), preferred_element_type=F32)
        fresh_b = jnp.dot(b_t, (wide * tail_b[:, one]).astype(BF16), preferred_element_type=F32)
        sf_ref[0, :, cols] = fresh_f
        sb_ref[0, :, cols] = fresh_b
        accf[:, cols] = accf[:, cols] * dec_f[:, one] + fresh_f
        accb[:, cols] = accb[:, cols] + run_b[1:2, one] * fresh_b
    run[...] = run_b * dec_ref[0]

    @pl.when(step == pl.num_programs(0) - 1)
    def _():
        part = LANES // GROUP
        for q in range(GROUP):
            tot_ref[q, 0] = accf[q * part:(q + 1) * part, :].astype(BF16)
            tot_ref[q, 1] = accb[q * part:(q + 1) * part, :].astype(BF16)
        totdec_ref[...] = run_b * dec_ref[0]


def local_part(xp, bc, halo, raw, bias, rate, aux, seg_rows, taps, taps_bc, heads):
    tok, inner = xp.shape
    blocks = tok // BLOCK
    part = LANES // GROUP
    row = lambda b: (b, 0)
    lead = lambda b: (b, 0, 0)
    fixed = lambda b: (0, 0)
    per = BLOCK // 16
    left = lambda b: (jnp.maximum(b * per - 1, 0), 0)
    right = lambda b: (jnp.minimum((b + 1) * per, tok // 16 - 1), 0)
    flops = tok * heads * (2 * BLOCK * LANES + 4 * LANES * LANES)
    return pl.pallas_call(
        functools.partial(local_kernel, heads),
        grid=(blocks,),
        in_specs=[
            pl.BlockSpec((BLOCK, inner), row),
            pl.BlockSpec((BLOCK, 2 * LANES), row),
            pl.BlockSpec((16, inner), left),
            pl.BlockSpec((16, inner), right),
            pl.BlockSpec((16, 2 * LANES), left),
            pl.BlockSpec((16, 2 * LANES), right),
            pl.BlockSpec((2, 16, inner + 2 * LANES), lambda b: (0, 0, 0)),
            pl.BlockSpec((BLOCK, LANES), row),
            pl.BlockSpec((1, LANES), fixed),
            pl.BlockSpec((1, LANES), fixed),
            pl.BlockSpec((BLOCK, 8), row),
            pl.BlockSpec((1, 1, BLOCK), lead),
            pl.BlockSpec((3, inner), fixed),
            pl.BlockSpec((3, 2 * LANES), fixed),
        ],
        out_specs=[
            pl.BlockSpec((BLOCK, inner), row),
            pl.BlockSpec((BLOCK, LANES), row),
            pl.BlockSpec((BLOCK, LANES), row),
            pl.BlockSpec((BLOCK, LANES), row),
            pl.BlockSpec((1, LANES, inner), lead),
            pl.BlockSpec((1, LANES, inner), lead),
            pl.BlockSpec((1, 8, LANES), lead),
            pl.BlockSpec((GROUP, 2, part, inner), lambda b: (0, 0, 0, 0)),
            pl.BlockSpec((8, LANES), fixed),
        ],
        out_shape=[
            jax.ShapeDtypeStruct((tok, inner), F32),
            jax.ShapeDtypeStruct((tok, LANES), BF16),
            jax.ShapeDtypeStruct((tok, LANES), F32),
            jax.ShapeDtypeStruct((tok, LANES), F32),
            jax.ShapeDtypeStruct((blocks, LANES, inner), F32),
            jax.ShapeDtypeStruct((blocks, LANES, inner), F32),
            jax.ShapeDtypeStruct((blocks, 8, LANES), F32),
            jax.ShapeDtypeStruct((GROUP, 2, part, inner), BF16),
            jax.ShapeDtypeStruct((8, LANES), F32),
        ],
        scratch_shapes=[
            pltpu.VMEM((LANES, inner), F32),
            pltpu.VMEM((LANES, inner), F32),
            pltpu.VMEM((8, LANES), F32),
        ],
        compiler_params=pltpu.CompilerParams(
            dimension_semantics=("arbitrary",), vmem_limit_bytes=VMEM_LIMIT
        ),
        cost_estimate=pl.CostEstimate(
            flops=flops, bytes_accessed=tok * inner * 6 + 4 * inner * LANES * 8,
            transcendentals=tok * BLOCK * heads,
        ),
        name="local_part",
    )(xp, bc, xp, xp, bc, bc, halo, raw, bias, rate, aux, seg_rows, taps, taps_bc)


def spread(row, heads):
    return jnp.concatenate(
        [jnp.broadcast_to(row[:, h:h + 1], (1, LANES)) for h in range(heads)], axis=1
    )


def product(terms):
    out = terms[0]
    for term in terms[1:]:
        out = out * term
    return out


def exchange_kernel(
    heads, zs, tot_ref, dec_ref, ent_ref,
    near, near_dec, sums, sums_dec, far_f, far_b, far_dec, back, landed,
    near_s, near_r, dec_s, dec_r, f_s, f_r, b_s, b_r, fd_s, fd_r, back_s, back_r,
):
    me = lax.axis_index("seq")
    i = lax.rem(me, GROUP)
    z = lax.div(me, GROUP)
    low, high = lax.rem(i, 2), lax.div(i, 2)
    members = [i]
    for r in range(1, GROUP):
        other_low = 1 - low if r % 2 else low
        other_high = 1 - high if r // 2 else high
        members.append(other_high * 2 + other_low)
    far_dec[...] = jnp.ones_like(far_dec)
    far_f[...] = jnp.zeros_like(far_f)
    far_b[...] = jnp.zeros_like(far_b)

    barrier = pltpu.get_barrier_semaphore()
    for r in range(1, GROUP):
        pl.semaphore_signal(
            barrier, inc=1, device_id={"seq": z * GROUP + members[r]}, device_id_type=MESH
        )
    for d in range(1, zs):
        pl.semaphore_signal(
            barrier, inc=1, device_id={"seq": lax.rem(z + d, zs) * GROUP + i}, device_id_type=MESH
        )
    pl.semaphore_wait(barrier, GROUP - 1 + zs - 1)

    def send(src, dst, ssem, rsem, to):
        return pltpu.make_async_remote_copy(
            src_ref=src, dst_ref=dst, send_sem=ssem, recv_sem=rsem,
            device_id={"seq": to}, device_id_type=MESH,
        )

    firsts = []
    for r in range(1, GROUP):
        to = z * GROUP + members[r]
        firsts.append(send(dec_ref, near_dec.at[r], dec_s.at[r], dec_r.at[r], to))
        firsts.append(send(tot_ref.at[members[r]], near.at[r], near_s.at[r], near_r.at[r], to))
    for copy in firsts:
        copy.start()
    for copy in firsts:
        copy.wait()

    decs = [dec_ref[...]] + [near_dec[r] for r in range(1, GROUP)]

    def state(r, way):
        value = tot_ref[i, way] if r == 0 else near[r, way]
        return value.astype(F32)

    def between(r, s, way):
        terms = []
        for k in range(GROUP):
            if way == 0:
                inside = (members[k] > members[r]) & (members[k] < members[s])
            else:
                inside = (members[k] < members[r]) & (members[k] > members[s])
            terms.append(jnp.where(inside, decs[k][way:way + 1], 1.0))
        return product(terms)

    def beyond(r, way):
        terms = []
        for k in range(GROUP):
            if way == 0:
                inside = members[k] > members[r]
            else:
                inside = members[k] < members[r]
            terms.append(jnp.where(inside, decs[k][way:way + 1], 1.0))
        return product(terms)

    for way in range(2):
        total = jnp.zeros(sums.shape[1:], F32)
        for r in range(GROUP):
            total = total + spread(beyond(r, way), heads) * state(r, way)
        sums[way] = total.astype(BF16)
    sums_dec[...] = product(decs)

    for d in range(1, zs):
        up = (z + d) * GROUP + i
        down = (z - d) * GROUP + i

        @pl.when(z + d < zs)
        def _():
            send(sums_dec, far_dec.at[0, d], fd_s.at[0, d], fd_r.at[0, d], up).start()
            send(sums.at[0], far_f.at[d], f_s.at[d], f_r.at[d], up).start()

        @pl.when(z - d >= 0)
        def _():
            send(sums_dec, far_dec.at[1, d], fd_s.at[1, d], fd_r.at[1, d], down).start()
            send(sums.at[1], far_b.at[d], b_s.at[d], b_r.at[d], down).start()

    for d in range(1, zs):
        up = (z + d) * GROUP + i
        down = (z - d) * GROUP + i

        @pl.when(z - d >= 0)
        def _():
            send(sums_dec, far_dec.at[0, d], fd_s.at[0, d], fd_r.at[0, d], down).wait_recv()
            send(sums.at[0], far_f.at[d], f_s.at[d], f_r.at[d], down).wait_recv()

        @pl.when(z + d < zs)
        def _():
            send(sums_dec, far_dec.at[1, d], fd_s.at[1, d], fd_r.at[1, d], up).wait_recv()
            send(sums.at[1], far_b.at[d], b_s.at[d], b_r.at[d], up).wait_recv()

    for way in range(2):
        far = far_b if way else far_f
        entering = jnp.zeros(sums.shape[1:], F32)
        weight = jnp.ones((1, LANES), F32)
        for d in range(1, zs):
            entering = entering + spread(weight, heads) * far[d].astype(F32)
            weight = weight * far_dec[way, d][way:way + 1]
        for s in range(GROUP):
            terms = []
            for k in range(GROUP):
                if way == 0:
                    earlier = members[k] < members[s]
                else:
                    earlier = members[k] > members[s]
                terms.append(jnp.where(earlier, decs[k][way:way + 1], 1.0))
            value = spread(product(terms), heads) * entering
            for r in range(GROUP):
                if r != s:
                    if way == 0:
                        earlier = members[r] < members[s]
                    else:
                        earlier = members[r] > members[s]
                    weight = jnp.where(earlier, between(r, s, way), 0.0)
                    value = value + spread(weight, heads) * state(r, way)
            back[s, way] = value.astype(BF16)

    lasts = []
    for r in range(1, GROUP):
        to = z * GROUP + members[r]
        lasts.append(send(back.at[r], landed.at[r], back_s.at[r], back_r.at[r], to))
    for copy in lasts:
        copy.start()
    ent_ref[i] = back[0]
    for r in range(1, GROUP):
        lasts[r - 1].wait()
        ent_ref[members[r]] = landed[r]

    for d in range(1, zs):
        up = (z + d) * GROUP + i
        down = (z - d) * GROUP + i

        @pl.when(z + d < zs)
        def _():
            send(sums_dec, far_dec.at[0, d], fd_s.at[0, d], fd_r.at[0, d], up).wait_send()
            send(sums.at[0], far_f.at[d], f_s.at[d], f_r.at[d], up).wait_send()

        @pl.when(z - d >= 0)
        def _():
            send(sums_dec, far_dec.at[1, d], fd_s.at[1, d], fd_r.at[1, d], down).wait_send()
            send(sums.at[1], far_b.at[d], b_s.at[d], b_r.at[d], down).wait_send()


def exchange(tot, totdec, heads):
    zs = lax.axis_size("seq") // GROUP
    _, _, part, inner = tot.shape
    dma = pltpu.SemaphoreType.DMA
    vmem = pl.BlockSpec(memory_space=pltpu.VMEM)
    return pl.pallas_call(
        functools.partial(exchange_kernel, heads, zs),
        in_specs=[vmem, vmem],
        out_specs=vmem,
        out_shape=jax.ShapeDtypeStruct(tot.shape, BF16),
        scratch_shapes=[
            pltpu.VMEM((GROUP, 2, part, inner), BF16),
            pltpu.VMEM((GROUP, 8, LANES), F32),
            pltpu.VMEM((2, part, inner), BF16),
            pltpu.VMEM((8, LANES), F32),
            pltpu.VMEM((zs, part, inner), BF16),
            pltpu.VMEM((zs, part, inner), BF16),
            pltpu.VMEM((2, zs, 8, LANES), F32),
            pltpu.VMEM((GROUP, 2, part, inner), BF16),
            pltpu.VMEM((GROUP, 2, part, inner), BF16),
            dma((GROUP,)), dma((GROUP,)), dma((GROUP,)), dma((GROUP,)),
            dma((zs,)), dma((zs,)), dma((zs,)), dma((zs,)),
            dma((2, zs)), dma((2, zs)),
            dma((GROUP,)), dma((GROUP,)),
        ],
        compiler_params=pltpu.CompilerParams(
            collective_id=1, has_side_effects=True, vmem_limit_bytes=VMEM_LIMIT
        ),
        cost_estimate=pl.CostEstimate(
            flops=tot.size * 20, bytes_accessed=tot.size * 8, transcendentals=0
        ),
        name="exchange_states",
    )(tot, totdec)


def finish_kernel(
    heads, inside_ref, c_ref, opf_ref, opb_ref, gate_ref, sf_ref, sb_ref, dec_ref, decs_ref,
    ent_ref, out_ref, sq_ref, hf, hb,
):
    step = pl.program_id(0)
    blocks = hb.shape[0]
    part = LANES // GROUP

    @pl.when(step == 0)
    def _():
        for q in range(GROUP):
            hf[q * part:(q + 1) * part, :] = ent_ref[q, 0].astype(F32)
        for h in range(heads):
            cols = slice(h * LANES, (h + 1) * LANES)
            now = jnp.concatenate([ent_ref[q, 1, :, cols] for q in range(GROUP)], axis=0).astype(F32)
            for b in range(blocks - 1, -1, -1):
                hb[b, :, cols] = now.astype(BF16)
                if b:
                    now = now * decs_ref[b, 1:2, h:h + 1] + sb_ref[b, :, cols]

    c_vecs = c_ref[...]
    opf, opb = opf_ref[...], opb_ref[...]
    squares = jnp.zeros((BLOCK, LANES), F32)
    for h in range(heads):
        cols = slice(h * LANES, (h + 1) * LANES)
        one = slice(h, h + 1)
        state = hf[:, cols]
        got_f = jnp.dot(c_vecs, state.astype(BF16), preferred_element_type=F32)
        got_b = jnp.dot(c_vecs, hb[step, :, cols], preferred_element_type=F32)
        hf[:, cols] = state * dec_ref[0, 0:1, one] + sf_ref[0, :, cols]
        mixed = inside_ref[:, cols] + got_f * opf[:, one] + got_b * opb[:, one]
        gated = mixed * silu(gate_ref[:, cols].astype(F32))
        squares = squares + gated * gated
        out_ref[:, cols] = gated
    sq_ref[...] = jnp.sum(squares, axis=1, keepdims=True)


def finish(inside, c_vecs, opf, opb, gate, sf, sb, dec, ent, heads):
    tok, inner = inside.shape
    blocks = tok // BLOCK
    part = LANES // GROUP
    row = lambda b: (b, 0)
    lead = lambda b: (b, 0, 0)
    whole = lambda b: (0, 0, 0)
    return pl.pallas_call(
        functools.partial(finish_kernel, heads),
        grid=(blocks,),
        in_specs=[
            pl.BlockSpec((BLOCK, inner), row),
            pl.BlockSpec((BLOCK, LANES), row),
            pl.BlockSpec((BLOCK, LANES), row),
            pl.BlockSpec((BLOCK, LANES), row),
            pl.BlockSpec((BLOCK, inner), row),
            pl.BlockSpec((1, LANES, inner), lead),
            pl.BlockSpec((blocks, LANES, inner), whole),
            pl.BlockSpec((1, 8, LANES), lead),
            pl.BlockSpec((blocks, 8, LANES), whole),
            pl.BlockSpec((GROUP, 2, part, inner), lambda b: (0, 0, 0, 0)),
        ],
        out_specs=[pl.BlockSpec((BLOCK, inner), row), pl.BlockSpec((BLOCK, 1), row)],
        out_shape=[
            jax.ShapeDtypeStruct((tok, inner), F32),
            jax.ShapeDtypeStruct((tok, 1), F32),
        ],
        scratch_shapes=[
            pltpu.VMEM((LANES, inner), F32),
            pltpu.VMEM((blocks, LANES, inner), BF16),
        ],
        compiler_params=pltpu.CompilerParams(
            dimension_semantics=("arbitrary",), vmem_limit_bytes=VMEM_LIMIT
        ),
        cost_estimate=pl.CostEstimate(
            flops=tok * inner * LANES * 4, bytes_accessed=tok * inner * 10, transcendentals=tok * inner
        ),
        name="finish",
    )(inside, c_vecs, opf, opb, gate, sf, sb, dec, dec, ent)


def neighbours(rows):
    count = lax.axis_size("seq")
    from_left = lax.ppermute(rows[-1:], "seq", [(i, i + 1) for i in range(count - 1)])
    from_right = lax.ppermute(rows[:1], "seq", [(i + 1, i) for i in range(count - 1)])
    return from_left, from_right


def shards(tokens, segment_ids, w_x, w_z, w_bc, w_dt, dt_bias, rates, conv_x, conv_bc, norm_gain):
    tok = tokens.shape[0]
    inner = w_x.shape[1]
    heads = w_dt.shape[1]
    mp_count = lax.axis_size("mp")
    seq_count = lax.axis_size("seq")
    position = lax.axis_index("seq")
    blocks = tok // BLOCK

    seg = segment_ids.astype(F32)
    seg_left, seg_right = neighbours(seg)
    seg_left = jnp.where(position > 0, seg_left, -1.0)
    seg_right = jnp.where(position < seq_count - 1, seg_right, -1.0)
    before = jnp.concatenate([seg_left, seg[:-1]])
    after = jnp.concatenate([seg[1:], seg_right])
    by_block = lambda v: jnp.repeat(v, BLOCK)
    aux = jnp.stack(
        [
            seg,
            (seg == before).astype(F32),
            (seg == after).astype(F32),
            (seg == by_block(before[::BLOCK])).astype(F32),
            (seg == by_block(after[BLOCK - 1::BLOCK])).astype(F32),
            (seg == by_block(seg[::BLOCK])).astype(F32),
            (seg == by_block(seg[BLOCK - 1::BLOCK])).astype(F32),
            seg,
        ],
        axis=1,
    )
    seg_rows = seg.reshape(blocks, 1, BLOCK)
    w_small = jnp.concatenate([w_bc, jnp.pad(w_dt, ((0, 0), (0, LANES - heads)))], axis=1)
    bias = jnp.pad(dt_bias, (0, LANES - heads))[None]
    rate = jnp.pad(rates, (0, LANES - heads))[None]

    xp, gate, bc, raw, halo = project(tokens, w_x, w_z, w_small)
    inside, c_vecs, opf, opb, sf, sb, dec, tot, totdec = local_part(
        xp, bc, halo, raw, bias, rate, aux, seg_rows, conv_x, conv_bc, heads
    )
    ent = exchange(tot, totdec, heads)
    gated, sq = finish(inside, c_vecs, opf, opb, gate, sf, sb, dec, ent, heads)
    squares = lax.psum(sq, "mp")
    scale = lax.rsqrt(squares / (inner * mp_count) + 1e-05)
    return (gated * scale * norm_gain).astype(BF16)


def solution(mesh):
    placed = (
        P("seq", "mp"),
        P("seq"),
        P(None, "mp"),
        P(None, "mp"),
        P(),
        P(None, "mp"),
        P("mp"),
        P("mp"),
        P(None, "mp"),
        P(),
        P("mp"),
    )
    return jax.shard_map(
        shards, mesh=mesh, in_specs=placed, out_specs=P("seq", "mp"), check_vma=False
    )
```

```python
import functools

import jax
import jax.numpy as jnp
from jax import lax
from jax.experimental import pallas as pl
from jax.experimental.pallas import tpu as pltpu
from jax.sharding import PartitionSpec as P

BLOCK = 256
LANES = 128
GROUP = 4
LOG2E = 1.4426950408889634
MESH = pl.DeviceIdType.MESH
VMEM_LIMIT = 60 * 1024 * 1024
F32 = jnp.float32
BF16 = jnp.bfloat16


TILE = 512


def project_kernel(
    mp, seqs, tok_ref, wx_ref, wz_ref, wbc_ref, wdt_ref,
    xp_ref, gate_ref, bc_ref, raw_ref, halo_ref,
    tok_v, wx_v, wz_v, ws_v, acc_x, acc_z, acc_s, stage_x, stage_z, edges, landed,
    own_sem, w_sem, send_sem, recv_sem, out_sem, edge_s, edge_r,
):
    me = lax.axis_index("mp")
    at = lax.axis_index("seq")
    tok, width = tok_ref.shape
    chunks = tok // BLOCK
    order = [0, chunks - 1] + list(range(1, chunks - 1))

    def rows(c):
        return pl.ds(c * BLOCK, BLOCK)

    loads = [
        pltpu.make_async_copy(src, dst, w_sem.at[n])
        for n, (src, dst) in enumerate(
            (
                (wx_ref, wx_v),
                (wbc_ref, ws_v.at[:, :2 * LANES]),
                (wdt_ref, ws_v.at[:, 2 * LANES:]),
                (wz_ref, wz_v),
            )
        )
    ]
    owns = [
        pltpu.make_async_copy(tok_ref.at[rows(c)], tok_v.at[me, rows(c)], own_sem.at[c])
        for c in range(chunks)
    ]
    barrier = pltpu.get_barrier_semaphore()
    for k in range(1, mp):
        pl.semaphore_signal(
            barrier, inc=1, device_id={"mp": lax.rem(me + k, mp)}, device_id_type=MESH
        )

    for other in (lax.rem(at + 1, seqs), lax.rem(at + seqs - 1, seqs)):
        pl.semaphore_signal(barrier, inc=1, device_id={"seq": other}, device_id_type=MESH)
    owns[order[0]].start()
    loads[0].start()
    pl.semaphore_wait(barrier, mp - 1 + 2)

    def sends(c):
        return [
            pltpu.make_async_remote_copy(
                src_ref=tok_ref.at[rows(c)], dst_ref=tok_v.at[me, rows(c)],
                send_sem=send_sem.at[k, c], recv_sem=recv_sem.at[k, c],
                device_id={"mp": lax.rem(me + k, mp)}, device_id_type=MESH,
            )
            for k in range(1, mp)
        ]

    def arrival(c, k):
        source = lax.rem(me - k + mp, mp)
        return source, pltpu.make_async_remote_copy(
            src_ref=tok_ref.at[rows(c)], dst_ref=tok_v.at[source, rows(c)],
            send_sem=send_sem.at[k, c], recv_sem=recv_sem.at[k, c],
            device_id={"mp": source}, device_id_type=MESH,
        )

    def edge(way, to):
        return pltpu.make_async_remote_copy(
            src_ref=edges.at[way], dst_ref=landed.at[way],
            send_sem=edge_s.at[way], recv_sem=edge_r.at[way],
            device_id={"seq": to}, device_id_type=MESH,
        )

    going = sends(order[0])
    for copy in going:
        copy.start()
    for load in loads[1:]:
        load.start()
    for c in order[1:]:
        owns[c].start()

    def out(c, slot, which):
        stage, to = (stage_x, xp_ref) if which == 0 else (stage_z, gate_ref)
        return pltpu.make_async_copy(stage.at[slot], to.at[rows(c)], out_sem.at[which, slot])

    for n, c in enumerate(order):
        slot = n % 2

        def contract(source, weights, acc, stage, first, last):
            depth = pl.ds(pl.multiple_of(source * width, width), width)
            tile = min(TILE, weights.shape[1])

            @pl.loop(0, weights.shape[1] // tile)
            def _(t):
                cols = pl.ds(pl.multiple_of(t * tile, tile), tile)
                part = jnp.dot(
                    tok_v[source, rows(c), :], weights[depth, cols], preferred_element_type=F32
                )
                if not first:
                    part = part + acc[:, cols]
                if last:
                    stage[slot, :, cols] = part.astype(BF16)
                else:
                    acc[:, cols] = part

        def contract_small(source, first):
            depth = pl.ds(pl.multiple_of(source * width, width), width)
            part = jnp.dot(tok_v[source, rows(c), :], ws_v[depth, :], preferred_element_type=F32)
            acc_s[...] = part if first else acc_s[...] + part

        owns[c].wait()
        if n == 0:
            loads[0].wait()
        contract(me, wx_v, acc_x, stage_x, True, False)
        if n == 0:
            loads[1].wait()
            loads[2].wait()
        contract_small(me, True)
        if n == 0:
            loads[3].wait()
        contract(me, wz_v, acc_z, stage_z, True, False)
        for copy in going:
            copy.wait_send()
        if n + 1 < chunks:
            going = sends(order[n + 1])
            for copy in going:
                copy.start()
        if n >= 2:
            for which in range(2):
                out(order[n - 2], slot, which).wait()
        sources = []
        for k in range(1, mp):
            source, copy = arrival(c, k)
            copy.wait_recv()
            sources.append(source)
            contract(source, wx_v, acc_x, stage_x, False, k == mp - 1)
            contract_small(source, False)
        out(c, slot, 0).start()
        bc_ref[rows(c), :] = acc_s[:, :2 * LANES].astype(BF16)
        raw_ref[rows(c), :] = acc_s[:, 2 * LANES:]
        inner = stage_x.shape[2]
        if n == 0:
            edges[0, :, :inner] = stage_x[slot, :16, :]
            edges[0, :, inner:] = acc_s[:16, :2 * LANES].astype(BF16)
        if n == 1:
            edges[1, :, :inner] = stage_x[slot, BLOCK - 16:, :]
            edges[1, :, inner:] = acc_s[BLOCK - 16:, :2 * LANES].astype(BF16)

            @pl.when(at > 0)
            def _():
                edge(0, at - 1).start()

            @pl.when(at < seqs - 1)
            def _():
                edge(1, at + 1).start()

        for k, source in enumerate(sources):
            contract(source, wz_v, acc_z, stage_z, False, k == mp - 2)
        out(c, slot, 1).start()

    @pl.when(at > 0)
    def _():
        edge(1, at - 1).wait_recv()
        halo_ref[0] = landed[1]
        edge(0, at - 1).wait_send()

    @pl.when(at == 0)
    def _():
        halo_ref[0] = jnp.zeros(halo_ref.shape[1:], BF16)

    @pl.when(at < seqs - 1)
    def _():
        edge(0, at + 1).wait_recv()
        halo_ref[1] = landed[0]
        edge(1, at + 1).wait_send()

    @pl.when(at == seqs - 1)
    def _():
        halo_ref[1] = jnp.zeros(halo_ref.shape[1:], BF16)

    for n in range(max(0, chunks - 2), chunks):
        for which in range(2):
            out(order[n], n % 2, which).wait()


def project(tokens, w_x, w_z, w_bc, w_steps):
    tok, width = tokens.shape
    inner = w_x.shape[1]
    mp = lax.axis_size("mp")
    seqs = lax.axis_size("seq")
    chunks = tok // BLOCK
    dma = pltpu.SemaphoreType.DMA
    anywhere = pl.BlockSpec(memory_space=pl.ANY)
    vmem = pl.BlockSpec(memory_space=pltpu.VMEM)
    small = w_bc.shape[1] + w_steps.shape[1]
    return pl.pallas_call(
        functools.partial(project_kernel, mp, seqs),
        in_specs=[anywhere] * 5,
        out_specs=[anywhere, anywhere, vmem, vmem, vmem],
        out_shape=[
            jax.ShapeDtypeStruct((tok, inner), BF16),
            jax.ShapeDtypeStruct((tok, inner), BF16),
            jax.ShapeDtypeStruct((tok, 2 * LANES), BF16),
            jax.ShapeDtypeStruct((tok, small - 2 * LANES), F32),
            jax.ShapeDtypeStruct((2, 16, inner + 2 * LANES), BF16),
        ],
        scratch_shapes=[
            pltpu.VMEM((mp, tok, width), BF16),
            pltpu.VMEM(w_x.shape, BF16),
            pltpu.VMEM(w_z.shape, BF16),
            pltpu.VMEM((w_x.shape[0], small), BF16),
            pltpu.VMEM((BLOCK, inner), F32),
            pltpu.VMEM((BLOCK, inner), F32),
            pltpu.VMEM((BLOCK, small), F32),
            pltpu.VMEM((2, BLOCK, inner), BF16),
            pltpu.VMEM((2, BLOCK, inner), BF16),
            pltpu.VMEM((2, 16, inner + 2 * LANES), BF16),
            pltpu.VMEM((2, 16, inner + 2 * LANES), BF16),
            dma((chunks,)), dma((4,)), dma((mp, chunks)), dma((mp, chunks)), dma((2, 2)),
            dma((2,)), dma((2,)),
        ],
        compiler_params=pltpu.CompilerParams(
            collective_id=2, has_side_effects=True, vmem_limit_bytes=VMEM_LIMIT
        ),
        cost_estimate=pl.CostEstimate(
            flops=2 * tok * width * mp * (2 * inner + small),
            bytes_accessed=width * mp * (2 * inner + small) * 2, transcendentals=0,
        ),
        name="gather_and_project",
    )(tokens, w_x, w_z, w_bc, w_steps)


def silu(v):
    return v / (1.0 + jnp.exp(-v))


def filtered(x, prev, nxt, m_prev, m_next, taps):
    rows = lax.broadcasted_iota(jnp.int32, x.shape, 0)
    last = x.shape[0] - 1
    before = jnp.where(rows == 0, prev, pltpu.roll(x, 1, axis=0)) * m_prev
    after = jnp.where(rows == last, nxt, pltpu.roll(x, last, axis=0)) * m_next
    return silu(taps[0:1] * before + taps[1:2] * x + taps[2:3] * after).astype(BF16)


def local_kernel(
    heads, x_ref, bc_ref, xl_ref, xr_ref, bl_ref, br_ref, halo_ref, raw_ref, bias_ref, rate_ref, aux_ref, seg_ref,
    taps_ref, taps_bc_ref,
    inside_ref, c_ref, opf_ref, opb_ref, sf_ref, sb_ref, dec_ref, tot_ref, totdec_ref,
    accf, accb, run,
):
    step = pl.program_id(0)
    inner = heads * LANES

    @pl.when(step == 0)
    def _():
        accf[...] = jnp.zeros_like(accf)
        accb[...] = jnp.zeros_like(accb)
        run[...] = jnp.ones_like(run)

    at_left = step == 0
    at_right = step == pl.num_programs(0) - 1

    def beside(left, right, cols):
        left_halo, right_halo = halo_ref[0, :, cols], halo_ref[1, :, cols]
        prev = jnp.where(at_left, left_halo.astype(F32), left.astype(F32))[15:16]
        nxt = jnp.where(at_right, right_halo.astype(F32), right.astype(F32))[0:1]
        return prev, nxt

    aux = aux_ref[...]
    seg_col, m_prev, m_next = aux[:, 0:1], aux[:, 1:2], aux[:, 2:3]
    from_prev, from_next = aux[:, 3:4], aux[:, 4:5]
    with_first, with_last = aux[:, 5:6], aux[:, 6:7]

    raw = raw_ref[...] + bias_ref[...]
    dt = jnp.maximum(raw, 0.0) + jnp.log1p(jnp.exp(-jnp.abs(raw)))
    drop = dt * (rate_ref[...] * -LOG2E)
    row_at = lax.broadcasted_iota(jnp.int32, (BLOCK, BLOCK), 0)
    col_at = lax.broadcasted_iota(jnp.int32, (BLOCK, BLOCK), 1)
    lower = col_at <= row_at
    incl = jnp.dot(lower.astype(F32), drop, precision=lax.Precision.HIGHEST, preferred_element_type=F32)
    excl = jnp.dot((col_at < row_at).astype(F32), drop, precision=lax.Precision.HIGHEST, preferred_element_type=F32)
    total = incl[BLOCK - 1:BLOCK]
    opf_ref[...] = jnp.exp2(incl) * from_prev
    opb_ref[...] = jnp.exp2(total - excl) * from_next
    tail_f = jnp.exp2(total - incl) * with_last * dt
    tail_b = jnp.exp2(excl) * with_first * dt
    whole = jnp.exp2(total)
    dec_f = whole * from_prev[BLOCK - 1:BLOCK]
    dec_b = whole * from_next[0:1]
    dec_ref[0] = jnp.concatenate([dec_f, dec_b, jnp.zeros((6, LANES), F32)], axis=0)
    incl_t, excl_t, dt_t = incl.T, excl.T, dt.T

    prev, nxt = beside(bl_ref[...], br_ref[...], slice(inner, inner + 2 * LANES))
    bcs = filtered(bc_ref[...].astype(F32), prev, nxt, m_prev, m_next, taps_bc_ref[...])
    c_vecs = bcs[:, LANES:]
    c_ref[...] = c_vecs
    b_t = bcs[:, :LANES].astype(F32).T.astype(BF16)
    scores = jnp.dot(c_vecs, b_t, preferred_element_type=F32)
    scores = jnp.where(seg_col == seg_ref[0], scores, 0.0)

    run_b = run[...]
    for h in range(heads):
        cols = slice(h * LANES, (h + 1) * LANES)
        prev, nxt = beside(xl_ref[:, cols], xr_ref[:, cols], cols)
        xs = filtered(x_ref[:, cols].astype(F32), prev, nxt, m_prev, m_next, taps_ref[:, cols])
        one = slice(h, h + 1)
        gap = jnp.where(lower, incl[:, one] - incl_t[one], excl_t[one] - excl[:, one])
        weights = (scores * jnp.exp2(gap) * dt_t[one]).astype(BF16)
        inside_ref[:, cols] = jnp.dot(weights, xs, preferred_element_type=F32)
        wide = xs.astype(F32)
        fresh_f = jnp.dot(b_t, (wide * tail_f[:, one]).astype(BF16), preferred_element_type=F32)
        fresh_b = jnp.dot(b_t, (wide * tail_b[:, one]).astype(BF16), preferred_element_type=F32)
        sf_ref[0, :, cols] = fresh_f
        sb_ref[0, :, cols] = fresh_b
        accf[:, cols] = accf[:, cols] * dec_f[:, one] + fresh_f
        accb[:, cols] = accb[:, cols] + run_b[1:2, one] * fresh_b
    run[...] = run_b * dec_ref[0]

    @pl.when(step == pl.num_programs(0) - 1)
    def _():
        part = LANES // GROUP
        for q in range(GROUP):
            tot_ref[q, 0] = accf[q * part:(q + 1) * part, :].astype(BF16)
            tot_ref[q, 1] = accb[q * part:(q + 1) * part, :].astype(BF16)
        totdec_ref[...] = run_b * dec_ref[0]


def local_part(xp, bc, halo, raw, bias, rate, aux, seg_rows, taps, taps_bc, heads):
    tok, inner = xp.shape
    blocks = tok // BLOCK
    part = LANES // GROUP
    row = lambda b: (b, 0)
    lead = lambda b: (b, 0, 0)
    fixed = lambda b: (0, 0)
    per = BLOCK // 16
    left = lambda b: (jnp.maximum(b * per - 1, 0), 0)
    right = lambda b: (jnp.minimum((b + 1) * per, tok // 16 - 1), 0)
    flops = tok * heads * (2 * BLOCK * LANES + 4 * LANES * LANES)
    return pl.pallas_call(
        functools.partial(local_kernel, heads),
        grid=(blocks,),
        in_specs=[
            pl.BlockSpec((BLOCK, inner), row),
            pl.BlockSpec((BLOCK, 2 * LANES), row),
            pl.BlockSpec((16, inner), left),
            pl.BlockSpec((16, inner), right),
            pl.BlockSpec((16, 2 * LANES), left),
            pl.BlockSpec((16, 2 * LANES), right),
            pl.BlockSpec((2, 16, inner + 2 * LANES), lambda b: (0, 0, 0)),
            pl.BlockSpec((BLOCK, LANES), row),
            pl.BlockSpec((1, LANES), fixed),
            pl.BlockSpec((1, LANES), fixed),
            pl.BlockSpec((BLOCK, 8), row),
            pl.BlockSpec((1, 1, BLOCK), lead),
            pl.BlockSpec((3, inner), fixed),
            pl.BlockSpec((3, 2 * LANES), fixed),
        ],
        out_specs=[
            pl.BlockSpec((BLOCK, inner), row),
            pl.BlockSpec((BLOCK, LANES), row),
            pl.BlockSpec((BLOCK, LANES), row),
            pl.BlockSpec((BLOCK, LANES), row),
            pl.BlockSpec((1, LANES, inner), lead),
            pl.BlockSpec((1, LANES, inner), lead),
            pl.BlockSpec((1, 8, LANES), lead),
            pl.BlockSpec((GROUP, 2, part, inner), lambda b: (0, 0, 0, 0)),
            pl.BlockSpec((8, LANES), fixed),
        ],
        out_shape=[
            jax.ShapeDtypeStruct((tok, inner), F32),
            jax.ShapeDtypeStruct((tok, LANES), BF16),
            jax.ShapeDtypeStruct((tok, LANES), F32),
            jax.ShapeDtypeStruct((tok, LANES), F32),
            jax.ShapeDtypeStruct((blocks, LANES, inner), F32),
            jax.ShapeDtypeStruct((blocks, LANES, inner), F32),
            jax.ShapeDtypeStruct((blocks, 8, LANES), F32),
            jax.ShapeDtypeStruct((GROUP, 2, part, inner), BF16),
            jax.ShapeDtypeStruct((8, LANES), F32),
        ],
        scratch_shapes=[
            pltpu.VMEM((LANES, inner), F32),
            pltpu.VMEM((LANES, inner), F32),
            pltpu.VMEM((8, LANES), F32),
        ],
        compiler_params=pltpu.CompilerParams(
            dimension_semantics=("arbitrary",), vmem_limit_bytes=VMEM_LIMIT
        ),
        cost_estimate=pl.CostEstimate(
            flops=flops, bytes_accessed=tok * inner * 6 + 4 * inner * LANES * 8,
            transcendentals=tok * BLOCK * heads,
        ),
        name="local_part",
    )(xp, bc, xp, xp, bc, bc, halo, raw, bias, rate, aux, seg_rows, taps, taps_bc)


def spread(row, heads):
    return jnp.concatenate(
        [jnp.broadcast_to(row[:, h:h + 1], (1, LANES)) for h in range(heads)], axis=1
    )


def product(terms):
    out = terms[0]
    for term in terms[1:]:
        out = out * term
    return out


def exchange_kernel(
    heads, zs, tot_ref, dec_ref, ent_ref,
    near, near_dec, sums, sums_dec, far_f, far_b, far_dec, back, landed,
    near_s, near_r, dec_s, dec_r, f_s, f_r, b_s, b_r, fd_s, fd_r, back_s, back_r,
):
    me = lax.axis_index("seq")
    i = lax.rem(me, GROUP)
    z = lax.div(me, GROUP)
    low, high = lax.rem(i, 2), lax.div(i, 2)
    members = [i]
    for r in range(1, GROUP):
        other_low = 1 - low if r % 2 else low
        other_high = 1 - high if r // 2 else high
        members.append(other_high * 2 + other_low)
    far_dec[...] = jnp.ones_like(far_dec)
    far_f[...] = jnp.zeros_like(far_f)
    far_b[...] = jnp.zeros_like(far_b)

    barrier = pltpu.get_barrier_semaphore()
    for r in range(1, GROUP):
        pl.semaphore_signal(
            barrier, inc=1, device_id={"seq": z * GROUP + members[r]}, device_id_type=MESH
        )
    for d in range(1, zs):
        pl.semaphore_signal(
            barrier, inc=1, device_id={"seq": lax.rem(z + d, zs) * GROUP + i}, device_id_type=MESH
        )
    pl.semaphore_wait(barrier, GROUP - 1 + zs - 1)

    def send(src, dst, ssem, rsem, to):
        return pltpu.make_async_remote_copy(
            src_ref=src, dst_ref=dst, send_sem=ssem, recv_sem=rsem,
            device_id={"seq": to}, device_id_type=MESH,
        )

    def near_copy(r, way):
        return send(
            tot_ref.at[members[r], way], near.at[r, way], near_s.at[r, way], near_r.at[r, way],
            z * GROUP + members[r],
        )

    def dec_copy(r):
        return send(dec_ref, near_dec.at[r], dec_s.at[r], dec_r.at[r], z * GROUP + members[r])

    for r in range(1, GROUP):
        dec_copy(r).start()
    for way in range(2):
        for r in range(1, GROUP):
            near_copy(r, way).start()
    for r in range(1, GROUP):
        dec_copy(r).wait()

    decs = [dec_ref[...]] + [near_dec[r] for r in range(1, GROUP)]

    def state(r, way):
        value = tot_ref[i, way] if r == 0 else near[r, way]
        return value.astype(F32)

    def between(r, s, way):
        terms = []
        for k in range(GROUP):
            if way == 0:
                inside = (members[k] > members[r]) & (members[k] < members[s])
            else:
                inside = (members[k] < members[r]) & (members[k] > members[s])
            terms.append(jnp.where(inside, decs[k][way:way + 1], 1.0))
        return product(terms)

    def beyond(r, way):
        terms = []
        for k in range(GROUP):
            if way == 0:
                inside = members[k] > members[r]
            else:
                inside = members[k] < members[r]
            terms.append(jnp.where(inside, decs[k][way:way + 1], 1.0))
        return product(terms)

    sums_dec[...] = product(decs)

    def far_copies(way, d):
        to = (z + d if way == 0 else z - d) * GROUP + i
        ssem, rsem = (f_s, f_r) if way == 0 else (b_s, b_r)
        far = far_b if way else far_f
        return (
            send(sums_dec, far_dec.at[way, d], fd_s.at[way, d], fd_r.at[way, d], to),
            send(sums.at[way], far.at[d], ssem.at[d], rsem.at[d], to),
        )

    def sends_far(way, d):
        return z + d < zs if way == 0 else z - d >= 0

    def gets_far(way, d):
        return z - d >= 0 if way == 0 else z + d < zs

    for way in range(2):
        for r in range(1, GROUP):
            near_copy(r, way).wait()
        total = jnp.zeros(sums.shape[1:], F32)
        for r in range(GROUP):
            total = total + spread(beyond(r, way), heads) * state(r, way)
        sums[way] = total.astype(BF16)
        for d in range(1, zs):

            @pl.when(sends_far(way, d))
            def _():
                for copy in far_copies(way, d):
                    copy.start()

    def back_copy(r, way):
        return send(
            back.at[r, way], landed.at[r, way], back_s.at[r, way], back_r.at[r, way],
            z * GROUP + members[r],
        )

    for way in range(2):
        far = far_b if way else far_f
        for d in range(1, zs):

            @pl.when(gets_far(way, d))
            def _():
                for copy in far_copies(way, d):
                    copy.wait_recv()

        entering = jnp.zeros(sums.shape[1:], F32)
        weight = jnp.ones((1, LANES), F32)
        for d in range(1, zs):
            entering = entering + spread(weight, heads) * far[d].astype(F32)
            weight = weight * far_dec[way, d][way:way + 1]
        for s in range(GROUP):
            terms = []
            for k in range(GROUP):
                if way == 0:
                    earlier = members[k] < members[s]
                else:
                    earlier = members[k] > members[s]
                terms.append(jnp.where(earlier, decs[k][way:way + 1], 1.0))
            value = spread(product(terms), heads) * entering
            for r in range(GROUP):
                if r != s:
                    if way == 0:
                        earlier = members[r] < members[s]
                    else:
                        earlier = members[r] > members[s]
                    weight = jnp.where(earlier, between(r, s, way), 0.0)
                    value = value + spread(weight, heads) * state(r, way)
            back[s, way] = value.astype(BF16)

        for r in range(1, GROUP):
            back_copy(r, way).start()

    ent_ref[i] = back[0]
    for r in range(1, GROUP):
        for way in range(2):
            back_copy(r, way).wait()
        ent_ref[members[r]] = landed[r]
    for way in range(2):
        for d in range(1, zs):

            @pl.when(sends_far(way, d))
            def _():
                for copy in far_copies(way, d):
                    copy.wait_send()


def exchange(tot, totdec, heads):
    zs = lax.axis_size("seq") // GROUP
    _, _, part, inner = tot.shape
    dma = pltpu.SemaphoreType.DMA
    vmem = pl.BlockSpec(memory_space=pltpu.VMEM)
    return pl.pallas_call(
        functools.partial(exchange_kernel, heads, zs),
        in_specs=[vmem, vmem],
        out_specs=vmem,
        out_shape=jax.ShapeDtypeStruct(tot.shape, BF16),
        scratch_shapes=[
            pltpu.VMEM((GROUP, 2, part, inner), BF16),
            pltpu.VMEM((GROUP, 8, LANES), F32),
            pltpu.VMEM((2, part, inner), BF16),
            pltpu.VMEM((8, LANES), F32),
            pltpu.VMEM((zs, part, inner), BF16),
            pltpu.VMEM((zs, part, inner), BF16),
            pltpu.VMEM((2, zs, 8, LANES), F32),
            pltpu.VMEM((GROUP, 2, part, inner), BF16),
            pltpu.VMEM((GROUP, 2, part, inner), BF16),
            dma((GROUP, 2)), dma((GROUP, 2)), dma((GROUP,)), dma((GROUP,)),
            dma((zs,)), dma((zs,)), dma((zs,)), dma((zs,)),
            dma((2, zs)), dma((2, zs)),
            dma((GROUP, 2)), dma((GROUP, 2)),
        ],
        compiler_params=pltpu.CompilerParams(
            collective_id=1, has_side_effects=True, vmem_limit_bytes=VMEM_LIMIT
        ),
        cost_estimate=pl.CostEstimate(
            flops=tot.size * 20, bytes_accessed=tot.size * 8, transcendentals=0
        ),
        name="exchange_states",
    )(tot, totdec)


def finish_kernel(
    heads, mp, inside_ref, c_ref, opf_ref, opb_ref, gate_ref, sf_ref, sb_ref, dec_ref, decs_ref,
    ent_ref, gain_ref, out_ref, hf, hb, held, sums, sent, got,
):
    step = pl.program_id(0)
    blocks = hb.shape[0]
    me = lax.axis_index("mp")

    def send(k, b):
        return pltpu.make_async_remote_copy(
            src_ref=sums.at[0, b], dst_ref=sums.at[k, b],
            send_sem=sent.at[k, b], recv_sem=got.at[k, b],
            device_id={"mp": lax.rem(me + k, mp)}, device_id_type=MESH,
        )

    @pl.when(step == 0)
    def _():
        barrier = pltpu.get_barrier_semaphore()
        for k in range(1, mp):
            pl.semaphore_signal(
                barrier, inc=1, device_id={"mp": lax.rem(me + k, mp)}, device_id_type=MESH
            )
        pl.semaphore_wait(barrier, mp - 1)
    part = LANES // GROUP

    @pl.when(step == 0)
    def _():
        for q in range(GROUP):
            hf[q * part:(q + 1) * part, :] = ent_ref[q, 0].astype(F32)
        for h in range(heads):
            cols = slice(h * LANES, (h + 1) * LANES)
            now = jnp.concatenate([ent_ref[q, 1, :, cols] for q in range(GROUP)], axis=0).astype(F32)
            for b in range(blocks - 1, -1, -1):
                hb[b, :, cols] = now.astype(BF16)
                if b:
                    now = now * decs_ref[b, 1:2, h:h + 1] + sb_ref[b, :, cols]

    c_vecs = c_ref[...]
    opf, opb = opf_ref[...], opb_ref[...]
    squares = jnp.zeros((BLOCK, LANES), F32)
    for h in range(heads):
        cols = slice(h * LANES, (h + 1) * LANES)
        one = slice(h, h + 1)
        state = hf[:, cols]
        got_f = jnp.dot(c_vecs, state.astype(BF16), preferred_element_type=F32)
        got_b = jnp.dot(c_vecs, hb[step, :, cols], preferred_element_type=F32)
        hf[:, cols] = state * dec_ref[0, 0:1, one] + sf_ref[0, :, cols]
        mixed = inside_ref[:, cols] + got_f * opf[:, one] + got_b * opb[:, one]
        gated = mixed * silu(gate_ref[:, cols].astype(F32))
        squares = squares + gated * gated
        held[step, :, cols] = gated
    sums[0, step] = jnp.broadcast_to(jnp.sum(squares.T, axis=0, keepdims=True), (8, BLOCK))
    for k in range(1, mp):
        send(k, step).start()

    @pl.when(step == blocks - 1)
    def _():
        for b in range(blocks):
            total = sums[0, b]
            for k in range(1, mp):
                send(k, b).wait_recv()
                total = total + sums[k, b]
            scale = lax.rsqrt(total[0:1] / (heads * LANES * mp) + 1e-05)
            scale = jnp.broadcast_to(scale, (LANES, BLOCK)).T
            for h in range(heads):
                cols = slice(h * LANES, (h + 1) * LANES)
                value = held[b, :, cols] * scale * gain_ref[:, cols]
                out_ref[b * BLOCK:(b + 1) * BLOCK, cols] = value.astype(BF16)
        for b in range(blocks):
            for k in range(1, mp):
                send(k, b).wait_send()


def finish(inside, c_vecs, opf, opb, gate, sf, sb, dec, ent, gain, heads):
    tok, inner = inside.shape
    blocks = tok // BLOCK
    part = LANES // GROUP
    row = lambda b: (b, 0)
    lead = lambda b: (b, 0, 0)
    whole = lambda b: (0, 0, 0)
    mp = lax.axis_size("mp")
    return pl.pallas_call(
        functools.partial(finish_kernel, heads, mp),
        grid=(blocks,),
        in_specs=[
            pl.BlockSpec((BLOCK, inner), row),
            pl.BlockSpec((BLOCK, LANES), row),
            pl.BlockSpec((BLOCK, LANES), row),
            pl.BlockSpec((BLOCK, LANES), row),
            pl.BlockSpec((BLOCK, inner), row),
            pl.BlockSpec((1, LANES, inner), lead),
            pl.BlockSpec((blocks, LANES, inner), whole),
            pl.BlockSpec((1, 8, LANES), lead),
            pl.BlockSpec((blocks, 8, LANES), whole),
            pl.BlockSpec((GROUP, 2, part, inner), lambda b: (0, 0, 0, 0)),
            pl.BlockSpec((1, inner), lambda b: (0, 0)),
        ],
        out_specs=pl.BlockSpec((tok, inner), lambda b: (0, 0)),
        out_shape=jax.ShapeDtypeStruct((tok, inner), BF16),
        scratch_shapes=[
            pltpu.VMEM((LANES, inner), F32),
            pltpu.VMEM((blocks, LANES, inner), BF16),
            pltpu.VMEM((blocks, BLOCK, inner), F32),
            pltpu.VMEM((mp, blocks, 8, BLOCK), F32),
            pltpu.SemaphoreType.DMA((mp, blocks)),
            pltpu.SemaphoreType.DMA((mp, blocks)),
        ],
        compiler_params=pltpu.CompilerParams(
            dimension_semantics=("arbitrary",), vmem_limit_bytes=VMEM_LIMIT,
            collective_id=3, has_side_effects=True,
        ),
        cost_estimate=pl.CostEstimate(
            flops=tok * inner * LANES * 4, bytes_accessed=tok * inner * 10, transcendentals=tok * inner
        ),
        name="finish",
    )(inside, c_vecs, opf, opb, gate, sf, sb, dec, dec, ent, gain[None])


def neighbours(rows):
    count = lax.axis_size("seq")
    from_left = lax.ppermute(rows[-1:], "seq", [(i, i + 1) for i in range(count - 1)])
    from_right = lax.ppermute(rows[:1], "seq", [(i + 1, i) for i in range(count - 1)])
    return from_left, from_right


def shards(tokens, segment_ids, w_x, w_z, w_bc, w_dt, dt_bias, rates, conv_x, conv_bc, norm_gain):
    tok = tokens.shape[0]
    inner = w_x.shape[1]
    heads = w_dt.shape[1]
    seq_count = lax.axis_size("seq")
    position = lax.axis_index("seq")
    blocks = tok // BLOCK

    seg = segment_ids.astype(F32)
    seg_left, seg_right = neighbours(seg)
    seg_left = jnp.where(position > 0, seg_left, -1.0)
    seg_right = jnp.where(position < seq_count - 1, seg_right, -1.0)
    before = jnp.concatenate([seg_left, seg[:-1]])
    after = jnp.concatenate([seg[1:], seg_right])
    by_block = lambda v: jnp.repeat(v, BLOCK)
    aux = jnp.stack(
        [
            seg,
            (seg == before).astype(F32),
            (seg == after).astype(F32),
            (seg == by_block(before[::BLOCK])).astype(F32),
            (seg == by_block(after[BLOCK - 1::BLOCK])).astype(F32),
            (seg == by_block(seg[::BLOCK])).astype(F32),
            (seg == by_block(seg[BLOCK - 1::BLOCK])).astype(F32),
            seg,
        ],
        axis=1,
    )
    seg_rows = seg.reshape(blocks, 1, BLOCK)
    w_steps = jnp.pad(w_dt, ((0, 0), (0, LANES - heads)))
    bias = jnp.pad(dt_bias, (0, LANES - heads))[None]
    rate = jnp.pad(rates, (0, LANES - heads))[None]

    xp, gate, bc, raw, halo = project(tokens, w_x, w_z, w_bc, w_steps)
    inside, c_vecs, opf, opb, sf, sb, dec, tot, totdec = local_part(
        xp, bc, halo, raw, bias, rate, aux, seg_rows, conv_x, conv_bc, heads
    )
    ent = exchange(tot, totdec, heads)
    return finish(inside, c_vecs, opf, opb, gate, sf, sb, dec, ent, norm_gain, heads)


def solution(mesh):
    placed = (
        P("seq", "mp"),
        P("seq"),
        P(None, "mp"),
        P(None, "mp"),
        P(),
        P(None, "mp"),
        P("mp"),
        P("mp"),
        P(None, "mp"),
        P(),
        P("mp"),
    )
    return jax.shard_map(
        shards, mesh=mesh, in_specs=placed, out_specs=P("seq", "mp"), check_vma=False
    )
```

```python
import functools

import jax
import jax.numpy as jnp
from jax import lax
from jax.experimental import pallas as pl
from jax.experimental.pallas import tpu as pltpu
from jax.sharding import PartitionSpec as P

BLOCK = 256
LANES = 128
GROUP = 4
LOG2E = 1.4426950408889634
MESH = pl.DeviceIdType.MESH
VMEM_LIMIT = 60 * 1024 * 1024
F32 = jnp.float32
BF16 = jnp.bfloat16


TILE = 512


def project_kernel(
    mp, seqs, tok_ref, wx_ref, wz_ref, wbc_ref, wdt_ref, seg_ref,
    xp_ref, gate_ref, bc_ref, raw_ref, halo_ref,
    tok_v, wx_v, wz_v, wbc_v, wdt_v, acc_x, acc_z, acc_s, stage_x, stage_z, edges, landed,
    own_sem, w_sem, send_sem, recv_sem, out_sem, edge_s, edge_r,
):
    me = lax.axis_index("mp")
    at = lax.axis_index("seq")
    tok, width = tok_ref.shape
    chunks = tok // BLOCK
    order = [0, chunks - 1] + list(range(1, chunks - 1))

    def rows(c):
        return pl.ds(c * BLOCK, BLOCK)

    loads = [
        pltpu.make_async_copy(src, dst, w_sem.at[n])
        for n, (src, dst) in enumerate(
            (
                (wx_ref, wx_v),
                (wbc_ref, wbc_v),
                (wdt_ref, wdt_v),
                (wz_ref, wz_v),
            )
        )
    ]
    owns = [
        pltpu.make_async_copy(tok_ref.at[rows(c)], tok_v.at[me, rows(c)], own_sem.at[c])
        for c in range(chunks)
    ]
    barrier = pltpu.get_barrier_semaphore()
    for k in range(1, mp):
        pl.semaphore_signal(
            barrier, inc=1, device_id={"mp": lax.rem(me + k, mp)}, device_id_type=MESH
        )

    for other in (lax.rem(at + 1, seqs), lax.rem(at + seqs - 1, seqs)):
        pl.semaphore_signal(barrier, inc=1, device_id={"seq": other}, device_id_type=MESH)
    owns[order[0]].start()
    loads[0].start()
    pl.semaphore_wait(barrier, mp - 1 + 2)

    def half(c, part):
        return pl.ds(c * BLOCK + part * (BLOCK // 2), BLOCK // 2)

    def sends(c):
        return [
            pltpu.make_async_remote_copy(
                src_ref=tok_ref.at[half(c, part)], dst_ref=tok_v.at[me, half(c, part)],
                send_sem=send_sem.at[k, c, part], recv_sem=recv_sem.at[k, c, part],
                device_id={"mp": lax.rem(me + k, mp)}, device_id_type=MESH,
            )
            for part in range(2)
            for k in range(1, mp)
        ]

    def arrival(c, k):
        source = lax.rem(me - k + mp, mp)
        return source, [
            pltpu.make_async_remote_copy(
                src_ref=tok_ref.at[half(c, part)], dst_ref=tok_v.at[source, half(c, part)],
                send_sem=send_sem.at[k, c, part], recv_sem=recv_sem.at[k, c, part],
                device_id={"mp": source}, device_id_type=MESH,
            )
            for part in range(2)
        ]

    def edge(way, to):
        return pltpu.make_async_remote_copy(
            src_ref=edges.at[way], dst_ref=landed.at[way],
            send_sem=edge_s.at[way], recv_sem=edge_r.at[way],
            device_id={"seq": to}, device_id_type=MESH,
        )

    going = sends(order[0])
    for copy in going:
        copy.start()
    for load in loads[1:]:
        load.start()
    for c in order[1:]:
        owns[c].start()

    def out(c, slot, which):
        stage, to = (stage_x, xp_ref) if which == 0 else (stage_z, gate_ref)
        return pltpu.make_async_copy(stage.at[slot], to.at[rows(c)], out_sem.at[which, slot])

    for n, c in enumerate(order):
        slot = n % 2

        def contract(source, weights, acc, stage, first, last):
            depth = pl.ds(pl.multiple_of(source * width, width), width)
            tile = min(TILE, weights.shape[1])

            @pl.loop(0, weights.shape[1] // tile)
            def _(t):
                cols = pl.ds(pl.multiple_of(t * tile, tile), tile)
                part = jnp.dot(
                    tok_v[source, rows(c), :], weights[depth, cols], preferred_element_type=F32
                )
                if not first:
                    part = part + acc[:, cols]
                if last:
                    stage[slot, :, cols] = part.astype(BF16)
                else:
                    acc[:, cols] = part

        def contract_small(source, first):
            depth = pl.ds(pl.multiple_of(source * width, width), width)
            piece = tok_v[source, rows(c), :]
            part = jnp.concatenate(
                [
                    jnp.dot(piece, wbc_v[depth, :], preferred_element_type=F32),
                    lax.dot_general(
                        piece, wdt_v[:, depth], (((1,), (1,)), ((), ())), preferred_element_type=F32
                    ),
                ],
                axis=1,
            )
            acc_s[...] = part if first else acc_s[...] + part

        owns[c].wait()
        if n == 0:
            loads[0].wait()
        contract(me, wx_v, acc_x, stage_x, True, False)
        if n == 0:
            loads[1].wait()
            loads[2].wait()
        contract_small(me, True)
        if n == 0:
            loads[3].wait()
        contract(me, wz_v, acc_z, stage_z, True, False)
        coming = sends(order[n + 1]) if n + 1 < chunks else []
        for at_copy, copy in enumerate(going):
            copy.wait_send()
            if coming:
                coming[at_copy].start()
        going = coming
        if n >= 2:
            for which in range(2):
                out(order[n - 2], slot, which).wait()
        sources = []
        for k in range(1, mp):
            source, copies = arrival(c, k)
            for copy in copies:
                copy.wait_recv()
            sources.append(source)
            contract(source, wx_v, acc_x, stage_x, False, k == mp - 1)
            contract_small(source, False)
        out(c, slot, 0).start()
        bc_ref[rows(c), :] = acc_s[:, :2 * LANES].astype(BF16)
        raw_ref[rows(c), :] = acc_s[:, 2 * LANES:]
        inner = stage_x.shape[2]
        if n == 0:
            edges[0, :, inner + 2 * LANES:] = seg_ref[0]
            edges[0, :, :inner] = stage_x[slot, :16, :]
            edges[0, :, inner:inner + 2 * LANES] = acc_s[:16, :2 * LANES].astype(BF16)
        if n == 1:
            edges[1, :, inner + 2 * LANES:] = seg_ref[1]
            edges[1, :, :inner] = stage_x[slot, BLOCK - 16:, :]
            edges[1, :, inner:inner + 2 * LANES] = acc_s[BLOCK - 16:, :2 * LANES].astype(BF16)

            @pl.when(at > 0)
            def _():
                edge(0, at - 1).start()

            @pl.when(at < seqs - 1)
            def _():
                edge(1, at + 1).start()

        for k, source in enumerate(sources):
            contract(source, wz_v, acc_z, stage_z, False, k == mp - 2)
        out(c, slot, 1).start()

    @pl.when(at > 0)
    def _():
        edge(1, at - 1).wait_recv()
        halo_ref[0] = landed[1]
        edge(0, at - 1).wait_send()

    @pl.when(at == 0)
    def _():
        halo_ref[0] = jnp.zeros(halo_ref.shape[1:], BF16)
        halo_ref[0, :, halo_ref.shape[2] - LANES:] = jnp.full((16, LANES), -1.0, BF16)

    @pl.when(at < seqs - 1)
    def _():
        edge(0, at + 1).wait_recv()
        halo_ref[1] = landed[0]
        edge(1, at + 1).wait_send()

    @pl.when(at == seqs - 1)
    def _():
        halo_ref[1] = jnp.zeros(halo_ref.shape[1:], BF16)
        halo_ref[1, :, halo_ref.shape[2] - LANES:] = jnp.full((16, LANES), -1.0, BF16)

    for n in range(max(0, chunks - 2), chunks):
        for which in range(2):
            out(order[n], n % 2, which).wait()


def project(tokens, w_x, w_z, w_bc, w_steps, seg_edges):
    tok, width = tokens.shape
    inner = w_x.shape[1]
    mp = lax.axis_size("mp")
    seqs = lax.axis_size("seq")
    chunks = tok // BLOCK
    dma = pltpu.SemaphoreType.DMA
    anywhere = pl.BlockSpec(memory_space=pl.ANY)
    vmem = pl.BlockSpec(memory_space=pltpu.VMEM)
    small = w_bc.shape[1] + w_steps.shape[0]
    return pl.pallas_call(
        functools.partial(project_kernel, mp, seqs),
        in_specs=[anywhere] * 5 + [vmem],
        out_specs=[anywhere, anywhere, vmem, vmem, vmem],
        out_shape=[
            jax.ShapeDtypeStruct((tok, inner), BF16),
            jax.ShapeDtypeStruct((tok, inner), BF16),
            jax.ShapeDtypeStruct((tok, 2 * LANES), BF16),
            jax.ShapeDtypeStruct((tok, small - 2 * LANES), F32),
            jax.ShapeDtypeStruct((2, 16, inner + 3 * LANES), BF16),
        ],
        scratch_shapes=[
            pltpu.VMEM((mp, tok, width), BF16),
            pltpu.VMEM(w_x.shape, BF16),
            pltpu.VMEM(w_z.shape, BF16),
            pltpu.VMEM(w_bc.shape, BF16),
            pltpu.VMEM(w_steps.shape, BF16),
            pltpu.VMEM((BLOCK, inner), F32),
            pltpu.VMEM((BLOCK, inner), F32),
            pltpu.VMEM((BLOCK, small), F32),
            pltpu.VMEM((2, BLOCK, inner), BF16),
            pltpu.VMEM((2, BLOCK, inner), BF16),
            pltpu.VMEM((2, 16, inner + 3 * LANES), BF16),
            pltpu.VMEM((2, 16, inner + 3 * LANES), BF16),
            dma((chunks,)), dma((4,)), dma((mp, chunks, 2)), dma((mp, chunks, 2)), dma((2, 2)),
            dma((2,)), dma((2,)),
        ],
        compiler_params=pltpu.CompilerParams(
            collective_id=2, has_side_effects=True, vmem_limit_bytes=VMEM_LIMIT
        ),
        cost_estimate=pl.CostEstimate(
            flops=2 * tok * width * mp * (2 * inner + small),
            bytes_accessed=width * mp * (2 * inner + small) * 2, transcendentals=0,
        ),
        name="gather_and_project",
    )(tokens, w_x, w_z, w_bc, w_steps, seg_edges)


def silu(v):
    return v / (1.0 + jnp.exp(-v))


def filtered(x, prev, nxt, m_prev, m_next, taps):
    rows = lax.broadcasted_iota(jnp.int32, x.shape, 0)
    last = x.shape[0] - 1
    before = jnp.where(rows == 0, prev, pltpu.roll(x, 1, axis=0)) * m_prev
    after = jnp.where(rows == last, nxt, pltpu.roll(x, last, axis=0)) * m_next
    return silu(taps[0:1] * before + taps[1:2] * x + taps[2:3] * after).astype(BF16)


def local_kernel(
    heads, x_ref, bc_ref, xl_ref, xr_ref, bl_ref, br_ref, halo_ref, raw_ref, bias_ref, rate_ref, aux_ref, seg_ref,
    taps_ref, taps_bc_ref,
    inside_ref, c_ref, opf_ref, opb_ref, sf_ref, sb_ref, dec_ref, tot_ref, totdec_ref,
    accf, accb, run,
):
    step = pl.program_id(0)
    inner = heads * LANES

    @pl.when(step == 0)
    def _():
        accf[...] = jnp.zeros_like(accf)
        accb[...] = jnp.zeros_like(accb)
        run[...] = jnp.ones_like(run)

    at_left = step == 0
    at_right = step == pl.num_programs(0) - 1

    def beside(left, right, cols):
        left_halo, right_halo = halo_ref[0, :, cols], halo_ref[1, :, cols]
        prev = jnp.where(at_left, left_halo.astype(F32), left.astype(F32))[15:16]
        nxt = jnp.where(at_right, right_halo.astype(F32), right.astype(F32))[0:1]
        return prev, nxt

    aux = aux_ref[...]
    seg_col, m_prev, m_next = aux[:, 0:1], aux[:, 1:2], aux[:, 2:3]
    from_prev, from_next = aux[:, 3:4], aux[:, 4:5]
    with_first, with_last = aux[:, 5:6], aux[:, 6:7]

    raw = raw_ref[...] + bias_ref[...]
    dt = jnp.maximum(raw, 0.0) + jnp.log1p(jnp.exp(-jnp.abs(raw)))
    drop = dt * (rate_ref[...] * -LOG2E)
    row_at = lax.broadcasted_iota(jnp.int32, (BLOCK, BLOCK), 0)
    col_at = lax.broadcasted_iota(jnp.int32, (BLOCK, BLOCK), 1)
    lower = col_at <= row_at
    incl = jnp.dot(lower.astype(F32), drop, precision=lax.Precision.HIGHEST, preferred_element_type=F32)
    excl = jnp.dot((col_at < row_at).astype(F32), drop, precision=lax.Precision.HIGHEST, preferred_element_type=F32)
    total = incl[BLOCK - 1:BLOCK]
    opf_ref[...] = jnp.exp2(incl) * from_prev
    opb_ref[...] = jnp.exp2(total - excl) * from_next
    tail_f = jnp.exp2(total - incl) * with_last * dt
    tail_b = jnp.exp2(excl) * with_first * dt
    whole = jnp.exp2(total)
    dec_f = whole * from_prev[BLOCK - 1:BLOCK]
    dec_b = whole * from_next[0:1]
    dec_ref[0] = jnp.concatenate([dec_f, dec_b, jnp.zeros((6, LANES), F32)], axis=0)
    incl_t, excl_t, dt_t = incl.T, excl.T, dt.T

    prev, nxt = beside(bl_ref[...], br_ref[...], slice(inner, inner + 2 * LANES))
    bcs = filtered(bc_ref[...].astype(F32), prev, nxt, m_prev, m_next, taps_bc_ref[...])
    c_vecs = bcs[:, LANES:]
    c_ref[...] = c_vecs
    b_t = bcs[:, :LANES].astype(F32).T.astype(BF16)
    scores = jnp.dot(c_vecs, b_t, preferred_element_type=F32)
    scores = jnp.where(seg_col == seg_ref[0], scores, 0.0)

    run_b = run[...]
    for h in range(heads):
        cols = slice(h * LANES, (h + 1) * LANES)
        prev, nxt = beside(xl_ref[:, cols], xr_ref[:, cols], cols)
        xs = filtered(x_ref[:, cols].astype(F32), prev, nxt, m_prev, m_next, taps_ref[:, cols])
        one = slice(h, h + 1)
        gap = jnp.where(lower, incl[:, one] - incl_t[one], excl_t[one] - excl[:, one])
        weights = (scores * jnp.exp2(gap) * dt_t[one]).astype(BF16)
        inside_ref[:, cols] = jnp.dot(weights, xs, preferred_element_type=F32)
        wide = xs.astype(F32)
        fresh_f = jnp.dot(b_t, (wide * tail_f[:, one]).astype(BF16), preferred_element_type=F32)
        fresh_b = jnp.dot(b_t, (wide * tail_b[:, one]).astype(BF16), preferred_element_type=F32)
        sf_ref[0, :, cols] = fresh_f
        sb_ref[0, :, cols] = fresh_b
        accf[:, cols] = accf[:, cols] * dec_f[:, one] + fresh_f
        accb[:, cols] = accb[:, cols] + run_b[1:2, one] * fresh_b
    run[...] = run_b * dec_ref[0]

    @pl.when(step == pl.num_programs(0) - 1)
    def _():
        part = LANES // GROUP
        for q in range(GROUP):
            tot_ref[q, 0] = accf[q * part:(q + 1) * part, :].astype(BF16)
            tot_ref[q, 1] = accb[q * part:(q + 1) * part, :].astype(BF16)
        totdec_ref[...] = run_b * dec_ref[0]


def local_part(xp, bc, halo, raw, bias, rate, aux, seg_rows, taps, taps_bc, heads):
    tok, inner = xp.shape
    blocks = tok // BLOCK
    part = LANES // GROUP
    row = lambda b: (b, 0)
    lead = lambda b: (b, 0, 0)
    fixed = lambda b: (0, 0)
    per = BLOCK // 16
    left = lambda b: (jnp.maximum(b * per - 1, 0), 0)
    right = lambda b: (jnp.minimum((b + 1) * per, tok // 16 - 1), 0)
    flops = tok * heads * (2 * BLOCK * LANES + 4 * LANES * LANES)
    return pl.pallas_call(
        functools.partial(local_kernel, heads),
        grid=(blocks,),
        in_specs=[
            pl.BlockSpec((BLOCK, inner), row),
            pl.BlockSpec((BLOCK, 2 * LANES), row),
            pl.BlockSpec((16, inner), left),
            pl.BlockSpec((16, inner), right),
            pl.BlockSpec((16, 2 * LANES), left),
            pl.BlockSpec((16, 2 * LANES), right),
            pl.BlockSpec((2, 16, inner + 3 * LANES), lambda b: (0, 0, 0)),
            pl.BlockSpec((BLOCK, LANES), row),
            pl.BlockSpec((1, LANES), fixed),
            pl.BlockSpec((1, LANES), fixed),
            pl.BlockSpec((BLOCK, 8), row),
            pl.BlockSpec((1, 1, BLOCK), lead),
            pl.BlockSpec((3, inner), fixed),
            pl.BlockSpec((3, 2 * LANES), fixed),
        ],
        out_specs=[
            pl.BlockSpec((BLOCK, inner), row),
            pl.BlockSpec((BLOCK, LANES), row),
            pl.BlockSpec((BLOCK, LANES), row),
            pl.BlockSpec((BLOCK, LANES), row),
            pl.BlockSpec((1, LANES, inner), lead),
            pl.BlockSpec((1, LANES, inner), lead),
            pl.BlockSpec((1, 8, LANES), lead),
            pl.BlockSpec((GROUP, 2, part, inner), lambda b: (0, 0, 0, 0)),
            pl.BlockSpec((8, LANES), fixed),
        ],
        out_shape=[
            jax.ShapeDtypeStruct((tok, inner), F32),
            jax.ShapeDtypeStruct((tok, LANES), BF16),
            jax.ShapeDtypeStruct((tok, LANES), F32),
            jax.ShapeDtypeStruct((tok, LANES), F32),
            jax.ShapeDtypeStruct((blocks, LANES, inner), F32),
            jax.ShapeDtypeStruct((blocks, LANES, inner), F32),
            jax.ShapeDtypeStruct((blocks, 8, LANES), F32),
            jax.ShapeDtypeStruct((GROUP, 2, part, inner), BF16),
            jax.ShapeDtypeStruct((8, LANES), F32),
        ],
        scratch_shapes=[
            pltpu.VMEM((LANES, inner), F32),
            pltpu.VMEM((LANES, inner), F32),
            pltpu.VMEM((8, LANES), F32),
        ],
        compiler_params=pltpu.CompilerParams(
            dimension_semantics=("arbitrary",), vmem_limit_bytes=VMEM_LIMIT
        ),
        cost_estimate=pl.CostEstimate(
            flops=flops, bytes_accessed=tok * inner * 6 + 4 * inner * LANES * 8,
            transcendentals=tok * BLOCK * heads,
        ),
        name="local_part",
    )(xp, bc, xp, xp, bc, bc, halo, raw, bias, rate, aux, seg_rows, taps, taps_bc)


def spread(row, heads):
    return jnp.concatenate(
        [jnp.broadcast_to(row[:, h:h + 1], (1, LANES)) for h in range(heads)], axis=1
    )


def product(terms):
    out = terms[0]
    for term in terms[1:]:
        out = out * term
    return out


def exchange_kernel(
    heads, zs, tot_ref, dec_ref, ent_ref,
    near, near_dec, sums, sums_dec, far_f, far_b, far_dec, back, landed,
    near_s, near_r, dec_s, dec_r, f_s, f_r, b_s, b_r, fd_s, fd_r, back_s, back_r,
):
    me = lax.axis_index("seq")
    i = lax.rem(me, GROUP)
    z = lax.div(me, GROUP)
    low, high = lax.rem(i, 2), lax.div(i, 2)
    members = [i]
    for r in range(1, GROUP):
        other_low = 1 - low if r % 2 else low
        other_high = 1 - high if r // 2 else high
        members.append(other_high * 2 + other_low)
    far_dec[...] = jnp.ones_like(far_dec)
    far_f[...] = jnp.zeros_like(far_f)
    far_b[...] = jnp.zeros_like(far_b)

    barrier = pltpu.get_barrier_semaphore()
    for r in range(1, GROUP):
        pl.semaphore_signal(
            barrier, inc=1, device_id={"seq": z * GROUP + members[r]}, device_id_type=MESH
        )
    for d in range(1, zs):
        pl.semaphore_signal(
            barrier, inc=1, device_id={"seq": lax.rem(z + d, zs) * GROUP + i}, device_id_type=MESH
        )
    pl.semaphore_wait(barrier, GROUP - 1 + zs - 1)

    def send(src, dst, ssem, rsem, to):
        return pltpu.make_async_remote_copy(
            src_ref=src, dst_ref=dst, send_sem=ssem, recv_sem=rsem,
            device_id={"seq": to}, device_id_type=MESH,
        )

    def near_copy(r, way):
        return send(
            tot_ref.at[members[r], way], near.at[r, way], near_s.at[r, way], near_r.at[r, way],
            z * GROUP + members[r],
        )

    def dec_copy(r):
        return send(dec_ref, near_dec.at[r], dec_s.at[r], dec_r.at[r], z * GROUP + members[r])

    for r in range(1, GROUP):
        dec_copy(r).start()
    for way in range(2):
        for r in range(1, GROUP):
            near_copy(r, way).start()
    for r in range(1, GROUP):
        dec_copy(r).wait()

    decs = [dec_ref[...]] + [near_dec[r] for r in range(1, GROUP)]

    def state(r, way):
        value = tot_ref[i, way] if r == 0 else near[r, way]
        return value.astype(F32)

    def between(r, s, way):
        terms = []
        for k in range(GROUP):
            if way == 0:
                inside = (members[k] > members[r]) & (members[k] < members[s])
            else:
                inside = (members[k] < members[r]) & (members[k] > members[s])
            terms.append(jnp.where(inside, decs[k][way:way + 1], 1.0))
        return product(terms)

    def beyond(r, way):
        terms = []
        for k in range(GROUP):
            if way == 0:
                inside = members[k] > members[r]
            else:
                inside = members[k] < members[r]
            terms.append(jnp.where(inside, decs[k][way:way + 1], 1.0))
        return product(terms)

    sums_dec[...] = product(decs)

    def far_copies(way, d):
        to = (z + d if way == 0 else z - d) * GROUP + i
        ssem, rsem = (f_s, f_r) if way == 0 else (b_s, b_r)
        far = far_b if way else far_f
        return (
            send(sums_dec, far_dec.at[way, d], fd_s.at[way, d], fd_r.at[way, d], to),
            send(sums.at[way], far.at[d], ssem.at[d], rsem.at[d], to),
        )

    def sends_far(way, d):
        return z + d < zs if way == 0 else z - d >= 0

    def gets_far(way, d):
        return z - d >= 0 if way == 0 else z + d < zs

    for way in range(2):
        for r in range(1, GROUP):
            near_copy(r, way).wait()
        total = jnp.zeros(sums.shape[1:], F32)
        for r in range(GROUP):
            total = total + spread(beyond(r, way), heads) * state(r, way)
        sums[way] = total.astype(BF16)
        for d in range(1, zs):

            @pl.when(sends_far(way, d))
            def _():
                for copy in far_copies(way, d):
                    copy.start()

    def back_copy(r, way):
        return send(
            back.at[r, way], landed.at[r, way], back_s.at[r, way], back_r.at[r, way],
            z * GROUP + members[r],
        )

    for way in range(2):
        far = far_b if way else far_f
        for d in range(1, zs):

            @pl.when(gets_far(way, d))
            def _():
                for copy in far_copies(way, d):
                    copy.wait_recv()

        entering = jnp.zeros(sums.shape[1:], F32)
        weight = jnp.ones((1, LANES), F32)
        for d in range(1, zs):
            entering = entering + spread(weight, heads) * far[d].astype(F32)
            weight = weight * far_dec[way, d][way:way + 1]
        for s in range(GROUP):
            terms = []
            for k in range(GROUP):
                if way == 0:
                    earlier = members[k] < members[s]
                else:
                    earlier = members[k] > members[s]
                terms.append(jnp.where(earlier, decs[k][way:way + 1], 1.0))
            value = spread(product(terms), heads) * entering
            for r in range(GROUP):
                if r != s:
                    if way == 0:
                        earlier = members[r] < members[s]
                    else:
                        earlier = members[r] > members[s]
                    weight = jnp.where(earlier, between(r, s, way), 0.0)
                    value = value + spread(weight, heads) * state(r, way)
            back[s, way] = value.astype(BF16)

        for r in range(1, GROUP):
            back_copy(r, way).start()

    ent_ref[i] = back[0]
    for r in range(1, GROUP):
        for way in range(2):
            back_copy(r, way).wait()
        ent_ref[members[r]] = landed[r]
    for way in range(2):
        for d in range(1, zs):

            @pl.when(sends_far(way, d))
            def _():
                for copy in far_copies(way, d):
                    copy.wait_send()


def exchange(tot, totdec, heads):
    zs = lax.axis_size("seq") // GROUP
    _, _, part, inner = tot.shape
    dma = pltpu.SemaphoreType.DMA
    vmem = pl.BlockSpec(memory_space=pltpu.VMEM)
    return pl.pallas_call(
        functools.partial(exchange_kernel, heads, zs),
        in_specs=[vmem, vmem],
        out_specs=vmem,
        out_shape=jax.ShapeDtypeStruct(tot.shape, BF16),
        scratch_shapes=[
            pltpu.VMEM((GROUP, 2, part, inner), BF16),
            pltpu.VMEM((GROUP, 8, LANES), F32),
            pltpu.VMEM((2, part, inner), BF16),
            pltpu.VMEM((8, LANES), F32),
            pltpu.VMEM((zs, part, inner), BF16),
            pltpu.VMEM((zs, part, inner), BF16),
            pltpu.VMEM((2, zs, 8, LANES), F32),
            pltpu.VMEM((GROUP, 2, part, inner), BF16),
            pltpu.VMEM((GROUP, 2, part, inner), BF16),
            dma((GROUP, 2)), dma((GROUP, 2)), dma((GROUP,)), dma((GROUP,)),
            dma((zs,)), dma((zs,)), dma((zs,)), dma((zs,)),
            dma((2, zs)), dma((2, zs)),
            dma((GROUP, 2)), dma((GROUP, 2)),
        ],
        compiler_params=pltpu.CompilerParams(
            collective_id=1, has_side_effects=True, vmem_limit_bytes=VMEM_LIMIT
        ),
        cost_estimate=pl.CostEstimate(
            flops=tot.size * 20, bytes_accessed=tot.size * 8, transcendentals=0
        ),
        name="exchange_states",
    )(tot, totdec)


def finish_kernel(
    heads, mp, inside_ref, c_ref, opf_ref, opb_ref, gate_ref, sf_ref, sb_ref, dec_ref, decs_ref,
    ent_ref, gain_ref, out_ref, hf, hb, held, sums, sent, got,
):
    step = pl.program_id(0)
    blocks = hb.shape[0]
    me = lax.axis_index("mp")

    def send(k, b):
        return pltpu.make_async_remote_copy(
            src_ref=sums.at[0, b], dst_ref=sums.at[k, b],
            send_sem=sent.at[k, b], recv_sem=got.at[k, b],
            device_id={"mp": lax.rem(me + k, mp)}, device_id_type=MESH,
        )

    @pl.when(step == 0)
    def _():
        barrier = pltpu.get_barrier_semaphore()
        for k in range(1, mp):
            pl.semaphore_signal(
                barrier, inc=1, device_id={"mp": lax.rem(me + k, mp)}, device_id_type=MESH
            )
        pl.semaphore_wait(barrier, mp - 1)
    part = LANES // GROUP

    @pl.when(step == 0)
    def _():
        for q in range(GROUP):
            hf[q * part:(q + 1) * part, :] = ent_ref[q, 0].astype(F32)
        for h in range(heads):
            cols = slice(h * LANES, (h + 1) * LANES)
            now = jnp.concatenate([ent_ref[q, 1, :, cols] for q in range(GROUP)], axis=0).astype(F32)
            for b in range(blocks - 1, -1, -1):
                hb[b, :, cols] = now.astype(BF16)
                if b:
                    now = now * decs_ref[b, 1:2, h:h + 1] + sb_ref[b, :, cols]

    c_vecs = c_ref[...]
    opf, opb = opf_ref[...], opb_ref[...]
    squares = jnp.zeros((BLOCK, LANES), F32)
    for h in range(heads):
        cols = slice(h * LANES, (h + 1) * LANES)
        one = slice(h, h + 1)
        state = hf[:, cols]
        got_f = jnp.dot(c_vecs, state.astype(BF16), preferred_element_type=F32)
        got_b = jnp.dot(c_vecs, hb[step, :, cols], preferred_element_type=F32)
        hf[:, cols] = state * dec_ref[0, 0:1, one] + sf_ref[0, :, cols]
        mixed = inside_ref[:, cols] + got_f * opf[:, one] + got_b * opb[:, one]
        gated = mixed * silu(gate_ref[:, cols].astype(F32))
        squares = squares + gated * gated
        held[step, :, cols] = gated
    sums[0, step] = jnp.broadcast_to(jnp.sum(squares.T, axis=0, keepdims=True), (8, BLOCK))
    for k in range(1, mp):
        send(k, step).start()

    @pl.when(step == blocks - 1)
    def _():
        for b in range(blocks):
            total = sums[0, b]
            for k in range(1, mp):
                send(k, b).wait_recv()
                total = total + sums[k, b]
            scale = lax.rsqrt(total[0:1] / (heads * LANES * mp) + 1e-05)
            scale = jnp.broadcast_to(scale, (LANES, BLOCK)).T
            for h in range(heads):
                cols = slice(h * LANES, (h + 1) * LANES)
                value = held[b, :, cols] * scale * gain_ref[:, cols]
                out_ref[b * BLOCK:(b + 1) * BLOCK, cols] = value.astype(BF16)
        for b in range(blocks):
            for k in range(1, mp):
                send(k, b).wait_send()


def finish(inside, c_vecs, opf, opb, gate, sf, sb, dec, ent, gain, heads):
    tok, inner = inside.shape
    blocks = tok // BLOCK
    part = LANES // GROUP
    row = lambda b: (b, 0)
    lead = lambda b: (b, 0, 0)
    whole = lambda b: (0, 0, 0)
    mp = lax.axis_size("mp")
    return pl.pallas_call(
        functools.partial(finish_kernel, heads, mp),
        grid=(blocks,),
        in_specs=[
            pl.BlockSpec((BLOCK, inner), row),
            pl.BlockSpec((BLOCK, LANES), row),
            pl.BlockSpec((BLOCK, LANES), row),
            pl.BlockSpec((BLOCK, LANES), row),
            pl.BlockSpec((BLOCK, inner), row),
            pl.BlockSpec((1, LANES, inner), lead),
            pl.BlockSpec((blocks, LANES, inner), whole),
            pl.BlockSpec((1, 8, LANES), lead),
            pl.BlockSpec((blocks, 8, LANES), whole),
            pl.BlockSpec((GROUP, 2, part, inner), lambda b: (0, 0, 0, 0)),
            pl.BlockSpec((1, inner), lambda b: (0, 0)),
        ],
        out_specs=pl.BlockSpec((tok, inner), lambda b: (0, 0)),
        out_shape=jax.ShapeDtypeStruct((tok, inner), BF16),
        scratch_shapes=[
            pltpu.VMEM((LANES, inner), F32),
            pltpu.VMEM((blocks, LANES, inner), BF16),
            pltpu.VMEM((blocks, BLOCK, inner), F32),
            pltpu.VMEM((mp, blocks, 8, BLOCK), F32),
            pltpu.SemaphoreType.DMA((mp, blocks)),
            pltpu.SemaphoreType.DMA((mp, blocks)),
        ],
        compiler_params=pltpu.CompilerParams(
            dimension_semantics=("arbitrary",), vmem_limit_bytes=VMEM_LIMIT,
            collective_id=3, has_side_effects=True,
        ),
        cost_estimate=pl.CostEstimate(
            flops=tok * inner * LANES * 4, bytes_accessed=tok * inner * 10, transcendentals=tok * inner
        ),
        name="finish",
    )(inside, c_vecs, opf, opb, gate, sf, sb, dec, dec, ent, gain[None])


def shards(tokens, segment_ids, w_x, w_z, w_bc, w_dt, dt_bias, rates, conv_x, conv_bc, norm_gain):
    tok = tokens.shape[0]
    inner = w_x.shape[1]
    heads = w_dt.shape[1]
    blocks = tok // BLOCK

    seg = segment_ids.astype(F32)
    w_steps = jnp.pad(w_dt.T, ((0, LANES - heads), (0, 0)))
    bias = jnp.pad(dt_bias, (0, LANES - heads))[None]
    rate = jnp.pad(rates, (0, LANES - heads))[None]

    seg_edges = jnp.stack([seg[0], seg[-1]]).astype(BF16)[:, None, None]
    seg_edges = jnp.broadcast_to(seg_edges, (2, 16, LANES))
    xp, gate, bc, raw, halo = project(tokens, w_x, w_z, w_bc, w_steps, seg_edges)
    seg_left = halo[0, 15, inner + 2 * LANES:][:1].astype(F32)
    seg_right = halo[1, 0, inner + 2 * LANES:][:1].astype(F32)
    before = jnp.concatenate([seg_left, seg[:-1]])
    after = jnp.concatenate([seg[1:], seg_right])
    by_block = lambda v: jnp.repeat(v, BLOCK)
    aux = jnp.stack(
        [
            seg,
            (seg == before).astype(F32),
            (seg == after).astype(F32),
            (seg == by_block(before[::BLOCK])).astype(F32),
            (seg == by_block(after[BLOCK - 1::BLOCK])).astype(F32),
            (seg == by_block(seg[::BLOCK])).astype(F32),
            (seg == by_block(seg[BLOCK - 1::BLOCK])).astype(F32),
            seg,
        ],
        axis=1,
    )
    seg_rows = seg.reshape(blocks, 1, BLOCK)
    inside, c_vecs, opf, opb, sf, sb, dec, tot, totdec = local_part(
        xp, bc, halo, raw, bias, rate, aux, seg_rows, conv_x, conv_bc, heads
    )
    ent = exchange(tot, totdec, heads)
    return finish(inside, c_vecs, opf, opb, gate, sf, sb, dec, ent, norm_gain, heads)


def solution(mesh):
    placed = (
        P("seq", "mp"),
        P("seq"),
        P(None, "mp"),
        P(None, "mp"),
        P(),
        P(None, "mp"),
        P("mp"),
        P("mp"),
        P(None, "mp"),
        P(),
        P("mp"),
    )
    return jax.shard_map(
        shards, mesh=mesh, in_specs=placed, out_specs=P("seq", "mp"), check_vma=False
    )
```
